32 devices in a mesh: gx: 16 (over z, y, core), gy: 2 (over x).
Axes of the slice: x: 2, y: 2, z: 4, core: 2. Of those that a mesh axis runs over, the one named last changes fastest.
Arguments:
- gas_state: float32 [5, 128, 16, 256], P(None, 'gx', 'gy'), may hold values from -3 to 3
- pressure_guess: float32 [128, 16, 256], P('gx', 'gy'), may hold values from -6 to 6
- drop_motion: float32 [4, 16, 8192], P(None, 'gx', 'gy'), may hold values from -6 to 6
- drop_size: float32 [16, 8192], P('gx', 'gy'), may hold values from 0.5 to 2
- drop_cell: int32 [16, 8192], P('gx', 'gy'), may hold values from 0 to 16383
- drop_target: int32 [16, 8192], P('gx', 'gy'), may hold values from -1 to 4, as said below
- spray_on: int32 [16, 16], P('gx', 'gy'), may hold values 0 or 1
- spray_time: int32 [16, 16], P('gx', 'gy'), may hold values from 0 to 100
- spray_cell: int32 [16, 16], P('gx', 'gy'), may hold values from 0 to 16383
Outputs:
- gas_next: float32 [5, 128, 16, 256], P(None, 'gx', 'gy')
- pressure: float32 [128, 16, 256], P('gx', 'gy')
- drop_kept: float32 [5, 16, 8192], P(None, 'gx', 'gy')
- drop_arrived: float32 [4, 5, 16, 1024], P(None, None, 'gx', 'gy')
The draws below stay inside these ranges and needn't reach their ends.
Inputs may be any that keep to these rules, and one draw needn't show every extreme that they name: `drop_target`: in each device's 4096 slots at most 512 droplets have any one of the targets 0, 1, 2, 3, and on every device one of these targets has exactly 512.
All inputs are finite; a program needn't handle non-finite values. No bound on the sum of `spray_on` on one device may be relied on, other than what follows from the above.
Results may differ from the reference program's by a relative error of at most 0.00002.
Values sent between devices are 32-bit elements; how exact they have to be, the bound alone decides.
A program may use at most 128 MiB of HBM per device.

```python
import math
import jax
import jax.numpy as jnp

CX = 8
CY = 8
NZ = 256
PD = 4096
SP = 8
ITERS = 8
CAP = 512
NX = 128
NY = 16
N_GX = 16
N_GY = 2


def draw_drop_target(key, part):
    devices = N_GX * N_GY
    key_counts, key_full, key_stay, key_order = jax.random.split(key, 4)
    counts = jax.random.randint(key_counts, (devices, 4), CAP // 3, CAP + 1)
    full = jax.random.randint(key_full, (devices,), 0, 4)
    counts = jnp.where(jnp.arange(4)[None, :] == full[:, None], CAP, counts)
    stayers = jax.random.randint(key_stay, (devices,), 0, PD - 4 * CAP + 1)
    bounds = jnp.cumsum(counts, axis=1)
    slots = jnp.arange(PD, dtype=jnp.int32)
    which = jnp.sum((slots[None, :, None] >= bounds[:, None, :]).astype(jnp.int32), axis=2)
    alive = slots[None, :] < bounds[:, 3:4] + stayers[:, None]
    target = jnp.where(alive, which, -1)
    scores = jax.random.randint(key_order, (devices, PD), 0, 65536) * PD + slots[None, :]
    order = jnp.argsort(scores, axis=1)
    target = jnp.take_along_axis(target, order, axis=1)
    return target.reshape(N_GX, N_GY * PD).astype(jnp.int32)


def set_ends(entries, key, low, high):
    dims = entries.shape
    spot = [jax.random.randint(jax.random.fold_in(key, axis), (), 0, dims[axis]) for axis in range(len(dims))]
    entries = entries.at[tuple(spot)].set(low)
    longest = dims.index(max(dims))
    spot[longest] = (spot[longest] + 1) % dims[longest]
    return entries.at[tuple(spot)].set(high)


def levels(own_key, shape, cuts, smallest, high):
    def one(dim, parts):
        heights = jax.random.uniform(jax.random.fold_in(jax.random.fold_in(own_key, 6), dim), (parts,), jnp.float32, smallest / len(cuts), high / len(cuts))
        return jnp.repeat(jnp.exp(heights), shape[dim] // parts).reshape((-1,) + (1,) * (len(shape) - dim - 1))

    loudness = one(*cuts[0])
    for cut in cuts[1:]:
        loudness = loudness * one(*cut)
    return loudness


def bell_draw(own_key, dims, scale, limit, cuts=(), kind=jnp.bfloat16):
    values = scale * jax.random.normal(own_key, dims, jnp.float32)
    if cuts:
        values = values * levels(own_key, dims, cuts, -0.22, 0.18)
    return jnp.clip(values, -limit, limit).astype(kind)


def setup_inputs(seed: int = 0) -> dict:
    keys = jax.random.split(jax.random.key(seed), 10)
    gas_state = bell_draw(keys[0], (5, NX, NY, NZ), 0.5, 3.0, ((1, 16), (2, 2)), jnp.float32)
    pressure_guess = bell_draw(keys[1], (NX, NY, NZ), 1.0, 6.0, ((0, 16), (1, 2)), jnp.float32)
    drop_motion = bell_draw(keys[2], (4, N_GX, N_GY * PD), 1.0, 6.0, ((1, 16), (2, 2)), jnp.float32)
    drop_size = jnp.clip(jnp.exp(math.log(2.0) - 1.3862944 * jax.random.uniform(keys[3], (N_GX, N_GY * PD), jnp.float32) ** levels(keys[3], (N_GX, N_GY * PD), ((0, 16), (1, 2)), -0.2, 0.2)), 0.5, 2.0)
    drop_cell = set_ends(jax.random.randint(keys[4], (N_GX, N_GY * PD), 0, CX * CY * NZ), jax.random.fold_in(keys[4], 1), 0, (CX * CY * NZ) - 1).astype(jnp.int32)
    drop_target = draw_drop_target(jax.random.fold_in(keys[9], 71), 0)
    spray_on = set_ends((jax.random.randint(keys[6], (N_GX, N_GY * SP), 0, 2) < 1).astype(jnp.int32), jax.random.fold_in(keys[6], 1), 0, 1)
    spray_time = set_ends(jax.random.randint(keys[7], (N_GX, N_GY * SP), 0, 101), jax.random.fold_in(keys[7], 1), 0, 100).astype(jnp.int32)
    spray_cell = set_ends(jax.random.randint(keys[8], (N_GX, N_GY * SP), 0, CX * CY * NZ), jax.random.fold_in(keys[8], 1), 0, (CX * CY * NZ) - 1).astype(jnp.int32)
    return dict(gas_state=gas_state, pressure_guess=pressure_guess, drop_motion=drop_motion, drop_size=drop_size, drop_cell=drop_cell, drop_target=drop_target, spray_on=spray_on, spray_time=spray_time, spray_cell=spray_cell)


TIME_STEP = 0.2
DIFFUSION = 0.1
DRAG_TIME = 0.5
HEAT_TIME = 1.0
GRAVITY = 1.0
VAPOUR_RATE = 0.5
DRAG_COUPLING = 0.5
LATENT = 2.0
VAPOUR_YIELD = 1.0
SPRAY_RATE = 3.0
CLOCK = 100.0
SPRAY_RAMP = 50.0


def window(padded, along_x, along_y, along_z):
    a = padded.shape[-3] - 4
    b = padded.shape[-2] - 4
    c = padded.shape[-1] - 4
    return padded[..., 2 + along_x:2 + along_x + a, 2 + along_y:2 + along_y + b, 2 + along_z:2 + along_z + c]


def gradient(padded, along_x, along_y, along_z):
    near = window(padded, along_x, along_y, along_z) - window(padded, -along_x, -along_y, -along_z)
    far = window(padded, 2 * along_x, 2 * along_y, 2 * along_z) - window(padded, -2 * along_x, -2 * along_y, -2 * along_z)
    return (8.0 * near - far) / 12.0


def predict(padded):
    speed_x = window(padded[0], 0, 0, 0)
    speed_y = window(padded[1], 0, 0, 0)
    speed_z = window(padded[2], 0, 0, 0)
    results = []
    for field in range(padded.shape[0]):
        single = padded[field]
        centre = window(single, 0, 0, 0)
        laplace = window(single, 1, 0, 0) + window(single, -1, 0, 0) + window(single, 0, 1, 0)
        laplace = laplace + window(single, 0, -1, 0) + window(single, 0, 0, 1) + window(single, 0, 0, -1) - 6.0 * centre
        transport = speed_x * gradient(single, 1, 0, 0) + speed_y * gradient(single, 0, 1, 0) + speed_z * gradient(single, 0, 0, 1)
        results.append(centre + TIME_STEP * (DIFFUSION * laplace - transport))
    return jnp.stack(results)


def divergence(flow_x, flow_y, vertical):
    lifted = jnp.pad(vertical, ((0, 0), (0, 0), (1, 1)))
    spread = 0.5 * (flow_x[2:, 1:-1] - flow_x[:-2, 1:-1]) + 0.5 * (flow_y[1:-1, 2:] - flow_y[1:-1, :-2])
    spread = spread + 0.5 * (lifted[:, :, 2:] - lifted[:, :, :-2])
    return spread / TIME_STEP


def sweep(bordered, source):
    inner = bordered[1:-1, 1:-1]
    lifted = jnp.pad(inner, ((0, 0), (0, 0), (1, 1)))
    beside_all = bordered[2:, 1:-1] + bordered[:-2, 1:-1] + bordered[1:-1, 2:] + bordered[1:-1, :-2]
    beside_all = beside_all + lifted[:, :, 2:] + lifted[:, :, :-2]
    return (beside_all - source) / 6.0


def correct(star, bordered):
    inner = bordered[1:-1, 1:-1]
    lifted = jnp.pad(inner, ((0, 0), (0, 0), (1, 1)))
    flow_x = star[0] - TIME_STEP * 0.5 * (bordered[2:, 1:-1] - bordered[:-2, 1:-1])
    flow_y = star[1] - TIME_STEP * 0.5 * (bordered[1:-1, 2:] - bordered[1:-1, :-2])
    vertical = star[2] - TIME_STEP * 0.5 * (lifted[:, :, 2:] - lifted[:, :, :-2])
    return jnp.concatenate([jnp.stack([flow_x, flow_y, vertical]), star[3:]], axis=0)


def droplets(motion, diameter, local):
    excess = local[3] - motion[3]
    vapour = VAPOUR_RATE * diameter * jax.nn.sigmoid(excess)
    renewed = jnp.stack([
        motion[0] + TIME_STEP * (local[0] - motion[0]) / DRAG_TIME,
        motion[1] + TIME_STEP * (local[1] - motion[1]) / DRAG_TIME,
        motion[2] + TIME_STEP * ((local[2] - motion[2]) / DRAG_TIME - GRAVITY),
        motion[3] + TIME_STEP * excess / HEAT_TIME,
        diameter - TIME_STEP * vapour])
    sources = jnp.stack([DRAG_COUPLING * diameter * diameter * (motion[2] - local[2]), -LATENT * vapour, VAPOUR_YIELD * vapour])
    return renewed, sources


def spray(flags, times):
    ramp = jnp.clip((CLOCK - times.astype(jnp.float32)) / SPRAY_RAMP, 0.0, 1.0)
    strength = SPRAY_RATE * ramp * flags.astype(jnp.float32)
    return jnp.stack([-strength, -strength, jnp.zeros_like(strength)])


def locate(cells, per_device):
    column = jnp.arange(N_GY * per_device, dtype=jnp.int32)[None, :] // per_device
    row = jnp.arange(N_GX, dtype=jnp.int32)[:, None]
    at_x = row * CX + cells // (CY * NZ)
    at_y = column * CY + (cells // NZ) % CY
    at_z = cells % NZ
    return at_x, at_y, at_z


def reference(gas_state, pressure_guess, drop_motion, drop_size, drop_cell, drop_target, spray_on, spray_time, spray_cell):
    at_x, at_y, at_z = locate(drop_cell, PD)
    local = gas_state[:, at_x, at_y, at_z]
    renewed, drop_sources = droplets(drop_motion, drop_size, local)
    drop_sources = jnp.where((drop_target >= 0)[None], drop_sources, 0.0)
    sources = jnp.zeros((3, NX, NY, NZ), jnp.float32).at[:, at_x, at_y, at_z].add(drop_sources)
    head_x, head_y, head_z = locate(spray_cell, SP)
    sources = sources.at[:, head_x, head_y, head_z].add(spray(spray_on, spray_time))
    padded = jnp.pad(gas_state, ((0, 0), (2, 2), (2, 2), (2, 2)))
    star = predict(padded)
    star = jnp.concatenate([star[:2], star[2:] + TIME_STEP * sources], axis=0)
    flows = jnp.pad(star[:2], ((0, 0), (1, 1), (1, 1), (0, 0)))
    source = divergence(flows[0], flows[1], star[2])
    field = pressure_guess
    for turn in range(ITERS):
        field = sweep(jnp.pad(field, ((1, 1), (1, 1), (0, 0))), source)
    gas_next = correct(star, jnp.pad(field, ((1, 1), (1, 1), (0, 0))))
    target = drop_target.reshape(N_GX, N_GY, PD)
    records = renewed.reshape(5, N_GX, N_GY, PD)
    rows = jnp.arange(N_GX, dtype=jnp.int32)[:, None, None]
    columns = jnp.arange(N_GY, dtype=jnp.int32)[None, :, None]
    parcels = []
    for heading in range(4):
        chosen = target == heading
        order = jnp.cumsum(chosen.astype(jnp.int32), axis=2) - 1
        place = jnp.where(chosen, order, CAP)
        parcel = jnp.zeros((5, N_GX, N_GY, CAP + 1), jnp.float32).at[:, rows, columns, place].set(records)
        parcels.append(parcel[..., :CAP])
    arrived = jnp.stack([
        jnp.pad(parcels[0], ((0, 0), (1, 0), (0, 0), (0, 0)))[:, :-1],
        jnp.pad(parcels[1], ((0, 0), (0, 1), (0, 0), (0, 0)))[:, 1:],
        jnp.pad(parcels[2], ((0, 0), (0, 0), (1, 0), (0, 0)))[:, :, :-1],
        jnp.pad(parcels[3], ((0, 0), (0, 0), (0, 1), (0, 0)))[:, :, 1:]])
    drop_arrived = arrived.reshape(4, 5, N_GX, N_GY * CAP)
    drop_kept = jnp.where((drop_target == 4)[None], renewed, 0.0)
    return gas_next, field, drop_kept, drop_arrived
```

```python
import functools

import jax
import jax.numpy as jnp
from jax import lax
from jax.experimental import pallas as pl
from jax.experimental.pallas import tpu as pltpu
from jax.sharding import PartitionSpec as P

ITERS = 8
TIME_STEP = 0.2
DIFFUSION = 0.1
DRAG_TIME = 0.5
HEAT_TIME = 1.0
GRAVITY = 1.0
VAPOUR_RATE = 0.5
DRAG_COUPLING = 0.5
LATENT = 2.0
SPRAY_RATE = 3.0
CLOCK = 100.0
SPRAY_RAMP = 50.0

MESH = pl.DeviceIdType.MESH
F32 = jnp.float32
BF16 = jnp.bfloat16
CHUNK = 1024
NT = (((1,), (1,)), ((), ()))
SIDES = ((1, 0), (-1, 0), (0, 1), (0, -1))
AROUND = SIDES + ((1, 1), (1, -1), (-1, 1), (-1, -1))


def split(values):
    high = values.astype(BF16).astype(F32)
    return high, values - high


def droplet_kernel(
    gas, motion, size, cell, target, spray_on, spray_time, spray_cell,
    sources, parcels, kept, grid_pieces, summed, packed,
):
    slots = size.shape[1]
    rows = gas.shape[1] * gas.shape[2]
    depth = gas.shape[3]
    table = gas[0:4].reshape(4 * rows, depth)
    high, low = split(table)
    grid_pieces[...] = jnp.concatenate([high, low], axis=0).astype(BF16)
    summed[...] = jnp.zeros_like(summed)
    packed[...] = jnp.zeros_like(packed)
    upper = (
        lax.broadcasted_iota(jnp.int32, (256, 256), 0) <= lax.broadcasted_iota(jnp.int32, (256, 256), 1)
    ).astype(F32).astype(BF16)
    eight = lax.broadcasted_iota(jnp.int32, (8, 256), 0)

    def step(turn, carry):
        here = pl.ds(pl.multiple_of(turn * CHUNK, CHUNK), CHUNK)
        cells = cell[:, here]
        goal = target[:, here]
        diameter = size[:, here]
        moving = motion[:, 0, here]
        at_z = jnp.bitwise_and(cells, depth - 1)
        at_xy = lax.shift_right_logical(cells, depth.bit_length() - 1)
        hot_z = (lax.broadcasted_iota(jnp.int32, (depth, CHUNK), 0) == at_z).astype(F32).astype(BF16)
        in_xy = lax.broadcasted_iota(jnp.int32, (rows, CHUNK), 0) == at_xy
        hot_xy = in_xy.astype(F32)
        found = jnp.dot(grid_pieces[...], hot_z, preferred_element_type=F32)
        found = found[: 4 * rows] + found[4 * rows :]
        local = jnp.concatenate(
            [jnp.sum(found[f * rows : (f + 1) * rows] * hot_xy, axis=0, keepdims=True) for f in range(4)], axis=0
        )
        gap = local - moving
        field = lax.broadcasted_iota(jnp.int32, gap.shape, 0)
        pace = jnp.where(field == 3, TIME_STEP / HEAT_TIME, TIME_STEP / DRAG_TIME)
        fall = jnp.where(field == 2, TIME_STEP * GRAVITY, 0.0)
        carried = moving + pace * gap - fall
        vapour = VAPOUR_RATE * diameter * (1.0 / (1.0 + jnp.exp(-gap[3:4])))
        shrunk = diameter - TIME_STEP * vapour
        renewed = jnp.concatenate([carried, shrunk], axis=0)
        kept[:, 0, here] = jnp.where(goal == 4, renewed, 0.0)
        alive = goal >= 0
        drag = jnp.where(alive, -DRAG_COUPLING * diameter * diameter * gap[2:3], 0.0)
        vapour = jnp.where(alive, vapour, 0.0)
        drag_high, drag_low = split(drag)
        vapour_high, vapour_low = split(vapour)
        spread = jnp.concatenate(
            [hot_xy * drag_high, hot_xy * vapour_high, hot_xy * drag_low, hot_xy * vapour_low], axis=0
        ).astype(BF16)
        summed[...] += lax.dot_general(spread, hot_z, NT, preferred_element_type=F32)

        pieces = [(eight == goal[:, k * 256 : k * 256 + 256]).astype(F32) for k in range(CHUNK // 256)]
        counts = jnp.dot(jnp.concatenate(pieces, axis=0).astype(BF16), upper, preferred_element_type=F32)
        places = []
        for k, piece in enumerate(pieces):
            count = counts[8 * k : 8 * k + 8] + carry
            carry = count[:, 255:256]
            place = jnp.where(eight < 4, piece * (count + (512.0 * eight.astype(F32))), 0.0)
            places.append(jnp.sum(place, axis=0, keepdims=True))
        place = jnp.concatenate(places, axis=1).astype(jnp.int32) - 1
        hot_low = (
            lax.broadcasted_iota(jnp.int32, (256, CHUNK), 0) == jnp.bitwise_and(place, 255)
        ).astype(F32).astype(BF16)
        hot_high = (
            lax.broadcasted_iota(jnp.int32, (8, CHUNK), 0) == lax.shift_right_arithmetic(place, 8)
        ).astype(F32)
        top, rest = split(renewed)
        bundle = jnp.concatenate(
            [hot_high * top[f : f + 1] for f in range(5)] + [hot_high * rest[f : f + 1] for f in range(5)], axis=0
        ).astype(BF16)
        packed[...] += lax.dot_general(bundle, hot_low, NT, preferred_element_type=F32)
        return carry

    lax.fori_loop(0, slots // CHUNK, step, jnp.zeros((8, 1), F32))

    numbers = lax.broadcasted_iota(jnp.int32, (rows, depth), 0) * depth + lax.broadcasted_iota(
        jnp.int32, (rows, depth), 1
    )
    ramp = jnp.clip((CLOCK - spray_time[...].astype(F32)) / SPRAY_RAMP, 0.0, 1.0)
    strength = SPRAY_RATE * ramp * spray_on[...].astype(F32)
    spray = jnp.zeros((rows, depth), F32)
    for head in range(spray_on.shape[1]):
        spray += jnp.where(numbers == spray_cell[:, head : head + 1], strength[:, head : head + 1], 0.0)
    total = summed[...]
    drag = total[:rows] + total[2 * rows : 3 * rows]
    vapour = total[rows : 2 * rows] + total[3 * rows :]
    shape = gas.shape[1:]
    sources[0] = (TIME_STEP * (drag - spray)).reshape(shape)
    sources[1] = (TIME_STEP * (-LATENT * vapour - spray)).reshape(shape)
    sources[2] = (TIME_STEP * vapour).reshape(shape)
    bundle = packed[0:40] + packed[40:80]
    parcels[...] = jnp.zeros_like(parcels)
    for f in range(5):
        for way in range(4):
            for half in range(2):
                row = f * 8 + 2 * way + half
                parcels[way, f : f + 1, half * 256 : half * 256 + 256] = bundle[row : row + 1]


def flow_kernel(
    n_gx, n_gy,
    gas, guess, sources, parcels,
    gas_next, pressure, arrived,
    wide, tall, edge_send, edge_recv, around, region, swap, star, tall_v, u_halo, v_send, v_recv, landed,
    send_halo, recv_halo, send_star, recv_star, send_parcel, recv_parcel, send_sum, recv_sum, send_src, recv_src,
):
    me_x, me_y = lax.axis_index("gx"), lax.axis_index("gy")

    def exists(dx, dy):
        to_x, to_y = me_x + dx, me_y + dy
        return (to_x >= 0) & (to_x < n_gx) & (to_y >= 0) & (to_y < n_gy)

    def device(dx, dy):
        return {"gx": jnp.clip(me_x + dx, 0, n_gx - 1), "gy": jnp.clip(me_y + dy, 0, n_gy - 1)}

    def copy(src, dst, send, recv, spot, side):
        return pltpu.make_async_remote_copy(
            src_ref=src, dst_ref=dst, send_sem=send.at[spot], recv_sem=recv.at[spot],
            device_id=device(*side), device_id_type=MESH,
        )

    def start(copies, sides):
        for one, (dx, dy) in zip(copies, sides):
            pl.when(exists(dx, dy))(one.start)

    def receive(copies, sides):
        for one, (dx, dy) in zip(copies, sides):
            pl.when(exists(-dx, -dy))(one.wait_recv)

    def sent(copies, sides):
        for one, (dx, dy) in zip(copies, sides):
            pl.when(exists(dx, dy))(one.wait_send)

    barrier = pltpu.get_barrier_semaphore()
    for dx, dy in AROUND:
        @pl.when(exists(dx, dy))
        def _():
            pl.semaphore_signal(barrier, inc=1, device_id=device(dx, dy), device_id_type=MESH)

    wide[0:5, 2:10] = gas[...]
    wide[5, 2:10] = guess[...]
    for f in range(6):
        own = guess[...] if f == 5 else gas[f]
        tall[f, :, 8:16] = own
        edge_send[0, f] = own[:, 6:8]
        edge_send[1, f] = own[:, 0:2]

    @pl.when(~exists(-1, 0))
    def _():
        wide[:, 0:2] = jnp.zeros((6, 2, 8, 256), F32)
        u_halo[0] = jnp.zeros((8, 256), F32)

    @pl.when(~exists(1, 0))
    def _():
        wide[:, 10:12] = jnp.zeros((6, 2, 8, 256), F32)
        u_halo[1] = jnp.zeros((8, 256), F32)

    @pl.when(~exists(0, -1))
    def _():
        edge_recv[0] = jnp.zeros((6, 8, 2, 256), F32)
        v_recv[0] = jnp.zeros((8, 1, 256), F32)

    @pl.when(~exists(0, 1))
    def _():
        edge_recv[1] = jnp.zeros((6, 8, 2, 256), F32)
        v_recv[1] = jnp.zeros((8, 1, 256), F32)

    for way, (dx, dy) in enumerate(SIDES):
        @pl.when(~exists(-dx, -dy))
        def _():
            landed[way] = jnp.zeros((8, 512), F32)

    for dx, dy in AROUND:
        @pl.when(~exists(dx, dy))
        def _():
            spot = (pl.ds(8 + 8 * dx, 8), pl.ds(8 + 8 * dy, 8))
            around[spot] = jnp.zeros((8, 8, 256), F32)
            region[spot] = jnp.zeros((8, 8, 256), F32)

    pl.semaphore_wait(barrier, sum(exists(dx, dy).astype(jnp.int32) for dx, dy in AROUND))

    halo = [
        copy(wide.at[:, pl.ds(8, 2)], wide.at[:, pl.ds(0, 2)], send_halo, recv_halo, 0, SIDES[0]),
        copy(wide.at[:, pl.ds(2, 2)], wide.at[:, pl.ds(10, 2)], send_halo, recv_halo, 1, SIDES[1]),
        copy(edge_send.at[0], edge_recv.at[0], send_halo, recv_halo, 2, SIDES[2]),
        copy(edge_send.at[1], edge_recv.at[1], send_halo, recv_halo, 3, SIDES[3]),
    ]
    start(halo, SIDES)
    parcel = [
        copy(parcels.at[way], landed.at[way], send_parcel, recv_parcel, way, SIDES[way]) for way in range(4)
    ]
    start(parcel, SIDES)
    receive(halo, SIDES)

    along = lax.broadcasted_iota(jnp.int32, (1, 1, 256), 2)
    masks = {
        1: (along >= 1).astype(F32), 2: (along >= 2).astype(F32),
        -1: (along < 255).astype(F32), -2: (along < 254).astype(F32),
    }

    def below(values, by):
        return pltpu.roll(values, by % 256, 2) * masks[by]

    for f in range(6):
        tall[f, :, 6:8] = edge_recv[0, f]
        tall[f, :, 16:18] = edge_recv[1, f]

    pace = [gas[0], gas[1], gas[2]]
    for f in (0, 1, 2, 3, 4):
        centre = gas[f]
        near_x, near_x2 = wide[f, 3:11], wide[f, 1:9]
        near_y, near_y2 = tall[f, :, 9:17], tall[f, :, 7:15]
        near_z, near_z2 = below(centre, -1), below(centre, 1)
        laplace = near_x + near_x2 + near_y + near_y2 + near_z + near_z2 - 6.0 * centre
        slope_x = 8.0 * (near_x - near_x2) - (wide[f, 4:12] - wide[f, 0:8])
        slope_y = 8.0 * (near_y - near_y2) - (tall[f, :, 10:18] - tall[f, :, 6:14])
        slope_z = 8.0 * (near_z - near_z2) - (below(centre, -2) - below(centre, 2))
        transport = (pace[0] * slope_x + pace[1] * slope_y + pace[2] * slope_z) * (1.0 / 12.0)
        result = centre + TIME_STEP * (DIFFUSION * laplace - transport)
        if f >= 2:
            result = result + sources[f - 2]
        star[f] = result

    tall_v[:, 8:16] = star[1]
    v_send[0] = star[1, :, 7:8]
    v_send[1] = star[1, :, 0:1]
    edges = [
        copy(star.at[0, 7], u_halo.at[0], send_star, recv_star, 0, SIDES[0]),
        copy(star.at[0, 0], u_halo.at[1], send_star, recv_star, 1, SIDES[1]),
        copy(v_send.at[0], v_recv.at[0], send_star, recv_star, 2, SIDES[2]),
        copy(v_send.at[1], v_recv.at[1], send_star, recv_star, 3, SIDES[3]),
    ]
    start(edges, SIDES)

    own = (pl.ds(8, 8), pl.ds(8, 8))
    around[own] = (
        wide[5, 3:11] + wide[5, 1:9] + tall[5, :, 9:17] + tall[5, :, 7:15]
        + below(guess[...], 1) + below(guess[...], -1)
    )

    def blocks(buffer, send, recv):
        return [
            copy(
                buffer.at[own], buffer.at[pl.ds(8 - 8 * dx, 8), pl.ds(8 - 8 * dy, 8)],
                send, recv, spot, (dx, dy),
            )
            for spot, (dx, dy) in enumerate(AROUND)
        ]

    sums = blocks(around, send_sum, recv_sum)
    start(sums, AROUND)
    receive(edges, SIDES)
    tall_v[:, 7:8] = v_recv[0]
    tall_v[:, 16:17] = v_recv[1]
    speed = star[0]
    spread_x = jnp.concatenate([speed[1:8], u_halo[1:2]], axis=0) - jnp.concatenate(
        [u_halo[0:1], speed[0:7]], axis=0
    )
    lift = star[2]
    spread = spread_x + (tall_v[:, 9:17] - tall_v[:, 7:15]) + (below(lift, -1) - below(lift, 1))
    region[own] = spread * (0.5 / TIME_STEP)
    parts = blocks(region, send_src, recv_src)
    start(parts, AROUND)

    receive(parcel, SIDES)
    for way in range(4):
        arrived[way, :, 0, :] = landed[way, 0:5]

    receive(sums, AROUND)
    receive(parts, AROUND)

    row = lax.broadcasted_iota(jnp.int32, (1, 24, 256), 1)
    low_y, high_y = exists(0, -1).astype(F32), exists(0, 1).astype(F32)
    factor = jnp.where(row < 8, low_y, jnp.where(row < 16, 1.0, high_y)) * (1.0 / 6.0)
    factors = [factor * exists(-1, 0).astype(F32), factor, factor * exists(1, 0).astype(F32)]

    for x in range(0, 24, 4):
        swap[0, x : x + 4] = (around[x : x + 4] - region[x : x + 4]) * factors[x // 8]
    for turn in range(1, ITERS):
        old, new = swap.at[(turn - 1) % 2], swap.at[turn % 2]
        x = turn
        while x < 24 - turn:
            end = min(x + 4, 24 - turn, (x // 8 + 1) * 8)
            centre = old[x:end]
            total = old[x - 1 : end - 1] + old[x + 1 : end + 1]
            total = total + pltpu.roll(centre, 1, 1) + pltpu.roll(centre, 23, 1)
            total = total + below(centre, 1) + below(centre, -1)
            new[x:end] = (total - region[x:end]) * factors[x // 8]
            x = end

    last = swap.at[(ITERS - 1) % 2]
    final = last[8:16, 8:16]
    pressure[...] = final
    half = TIME_STEP * 0.5
    gas_next[0] = star[0] - half * (last[9:17, 8:16] - last[7:15, 8:16])
    gas_next[1] = star[1] - half * (last[8:16, 9:17] - last[8:16, 7:15])
    gas_next[2] = star[2] - half * (below(final, -1) - below(final, 1))
    gas_next[3] = star[3]
    gas_next[4] = star[4]

    sent(halo, SIDES)
    sent(parcel, SIDES)
    sent(edges, SIDES)
    sent(sums, AROUND)
    sent(parts, AROUND)


def body(
    n_gx, n_gy,
    gas_state, pressure_guess, drop_motion, drop_size, drop_cell, drop_target, spray_on, spray_time, spray_cell,
):
    vmem = pl.BlockSpec(memory_space=pltpu.VMEM)
    slots = drop_size.shape[1]
    block = gas_state.shape[1:]
    sources, parcels, kept = pl.pallas_call(
        droplet_kernel,
        out_shape=(
            jax.ShapeDtypeStruct((3,) + block, F32),
            jax.ShapeDtypeStruct((4, 8, 512), F32),
            jax.ShapeDtypeStruct((5, 1, slots), F32),
        ),
        in_specs=[vmem] * 8,
        out_specs=(vmem,) * 3,
        scratch_shapes=[
            pltpu.VMEM((512, 256), BF16),
            pltpu.VMEM((256, 256), F32),
            pltpu.VMEM((80, 256), F32),
        ],
        compiler_params=pltpu.CompilerParams(vmem_limit_bytes=40 * 1024 * 1024),
    )(gas_state, drop_motion, drop_size, drop_cell, drop_target, spray_on, spray_time, spray_cell)
    dma = pltpu.SemaphoreType.DMA
    gas_next, pressure, arrived = pl.pallas_call(
        functools.partial(flow_kernel, n_gx, n_gy),
        out_shape=(
            jax.ShapeDtypeStruct(gas_state.shape, F32),
            jax.ShapeDtypeStruct(block, F32),
            jax.ShapeDtypeStruct((4, 5, 1, 512), F32),
        ),
        in_specs=[vmem] * 4,
        out_specs=(vmem,) * 3,
        scratch_shapes=[
            pltpu.VMEM((6, 12, 8, 256), F32),
            pltpu.VMEM((6, 8, 24, 256), F32),
            pltpu.VMEM((2, 6, 8, 2, 256), F32),
            pltpu.VMEM((2, 6, 8, 2, 256), F32),
            pltpu.VMEM((24, 24, 256), F32),
            pltpu.VMEM((24, 24, 256), F32),
            pltpu.VMEM((2, 24, 24, 256), F32),
            pltpu.VMEM((5, 8, 8, 256), F32),
            pltpu.VMEM((8, 24, 256), F32),
            pltpu.VMEM((2, 8, 256), F32),
            pltpu.VMEM((2, 8, 1, 256), F32),
            pltpu.VMEM((2, 8, 1, 256), F32),
            pltpu.VMEM((4, 8, 512), F32),
        ]
        + [dma((4,))] * 6 + [dma((8,))] * 4,
        compiler_params=pltpu.CompilerParams(
            collective_id=0, has_side_effects=True, vmem_limit_bytes=40 * 1024 * 1024
        ),
    )(gas_state, pressure_guess, sources, parcels)
    return gas_next, pressure, kept, arrived


def solution(mesh):
    in_specs = (
        P(None, "gx", "gy", None),
        P("gx", "gy", None),
        P(None, "gx", "gy"),
    ) + (P("gx", "gy"),) * 6
    out_specs = (
        P(None, "gx", "gy", None),
        P("gx", "gy", None),
        P(None, "gx", "gy"),
        P(None, None, "gx", "gy"),
    )
    inner = functools.partial(body, mesh.shape["gx"], mesh.shape["gy"])
    return jax.shard_map(inner, mesh=mesh, in_specs=in_specs, out_specs=out_specs, check_vma=False)
```

```python
import functools

import jax
import jax.numpy as jnp
from jax import lax
from jax.experimental import pallas as pl
from jax.experimental.pallas import tpu as pltpu
from jax.sharding import PartitionSpec as P

ITERS = 8
TIME_STEP = 0.2
DIFFUSION = 0.1
DRAG_TIME = 0.5
HEAT_TIME = 1.0
GRAVITY = 1.0
VAPOUR_RATE = 0.5
DRAG_COUPLING = 0.5
LATENT = 2.0
SPRAY_RATE = 3.0
CLOCK = 100.0
SPRAY_RAMP = 50.0

MESH = pl.DeviceIdType.MESH
F32 = jnp.float32
BF16 = jnp.bfloat16
CHUNK = 1024
NT = (((1,), (1,)), ((), ()))
SIDES = ((1, 0), (-1, 0), (0, 1), (0, -1))
CORNERS = ((1, 1), (1, -1), (-1, 1), (-1, -1))
AROUND = SIDES + CORNERS


def split(values):
    high = values.astype(BF16).astype(F32)
    return high, values - high


def along_depth(values, by):
    place = lax.broadcasted_iota(jnp.int32, (1, 1, 256), 2)
    keep = place >= by if by > 0 else place < 256 + by
    return pltpu.roll(values, by % 256, 2) * keep.astype(F32)


def evolve_kernel(
    n_gx, n_gy,
    gas_hbm, guess_hbm, motion_hbm, size_hbm, cell_hbm, target_hbm, on_hbm, time_hbm, place_hbm,
    gas_next, pressure, kept_hbm, arrived_hbm,
    star, factors, kept, arrived, swap, final,
    motion, size, cell, target, spray_on, spray_time, spray_cell,
    grid_pieces, summed, packed, renewed, parcels, landed,
    wide, tall, edge_send, edge_recv, sums, parts, corner_send, corner_recv, tall_v, u_halo, v_send, v_recv,
    send_in, send_out, send_halo, recv_halo, send_star, recv_star, send_parcel, recv_parcel, send_sum, recv_sum, send_src,
    recv_src,
):
    me_x, me_y = lax.axis_index("gx"), lax.axis_index("gy")
    slots = size.shape[1]
    rows, depth = 64, 256

    def exists(dx, dy):
        to_x, to_y = me_x + dx, me_y + dy
        return (to_x >= 0) & (to_x < n_gx) & (to_y >= 0) & (to_y < n_gy)

    def device(dx, dy):
        return {"gx": jnp.clip(me_x + dx, 0, n_gx - 1), "gy": jnp.clip(me_y + dy, 0, n_gy - 1)}

    def copy(src, dst, send, recv, spot, side):
        return pltpu.make_async_remote_copy(
            src_ref=src, dst_ref=dst, send_sem=send.at[spot], recv_sem=recv.at[spot],
            device_id=device(*side), device_id_type=MESH,
        )

    def start(copies, sides):
        for one, (dx, dy) in zip(copies, sides):
            pl.when(exists(dx, dy))(one.start)

    def receive(copies, sides):
        for one, (dx, dy) in zip(copies, sides):
            pl.when(exists(-dx, -dy))(one.wait_recv)

    def sent(copies, sides):
        for one, (dx, dy) in zip(copies, sides):
            pl.when(exists(dx, dy))(one.wait_send)

    loads = [
        pltpu.make_async_copy(src, dst, send_in.at[spot])
        for spot, (src, dst) in enumerate(
            (
                (gas_hbm, wide.at[pl.ds(0, 5), pl.ds(2, 8)]),
                (guess_hbm, wide.at[5, pl.ds(2, 8)]),
                (gas_hbm, tall.at[pl.ds(0, 5), :, pl.ds(8, 8)]),
                (guess_hbm, tall.at[5, :, pl.ds(8, 8)]),
                (cell_hbm, cell),
                (motion_hbm, motion),
                (size_hbm, size),
                (target_hbm, target),
                (on_hbm, spray_on),
                (time_hbm, spray_time),
                (place_hbm, spray_cell),
            )
        )
    ]
    for one in loads:
        one.start()

    barrier = pltpu.get_barrier_semaphore()
    for dx, dy in AROUND:
        @pl.when(exists(dx, dy))
        def _():
            pl.semaphore_signal(barrier, inc=1, device_id=device(dx, dy), device_id_type=MESH)

    @pl.when(~exists(-1, 0))
    def _():
        wide[:, 0:2] = jnp.zeros((6, 2, 8, 256), F32)
        u_halo[0] = jnp.zeros((8, 256), F32)

    @pl.when(~exists(1, 0))
    def _():
        wide[:, 10:12] = jnp.zeros((6, 2, 8, 256), F32)
        u_halo[1] = jnp.zeros((8, 256), F32)

    @pl.when(~exists(0, -1))
    def _():
        edge_recv[0] = jnp.zeros((6, 8, 2, 256), F32)
        v_recv[0] = jnp.zeros((8, 1, 256), F32)

    @pl.when(~exists(0, 1))
    def _():
        edge_recv[1] = jnp.zeros((6, 8, 2, 256), F32)
        v_recv[1] = jnp.zeros((8, 1, 256), F32)

    for way, (dx, dy) in enumerate(SIDES):
        @pl.when(~exists(-dx, -dy))
        def _():
            spot = (pl.ds(8 - 8 * dx, 8), pl.ds(8 - 8 * dy, 8))
            landed[way] = jnp.zeros((8, 512), F32)
            sums[spot] = jnp.zeros((8, 8, 256), F32)
            parts[spot] = jnp.zeros((8, 8, 256), F32)

    for way, (dx, dy) in enumerate(CORNERS):
        @pl.when(~exists(-dx, -dy))
        def _():
            corner_recv[0, way] = jnp.zeros((4, 8, 256), F32)
            corner_recv[1, way] = jnp.zeros((4, 8, 256), F32)

    row = lax.broadcasted_iota(jnp.int32, (24, 256), 0)
    low_y, high_y = exists(0, -1).astype(F32), exists(0, 1).astype(F32)
    factor = jnp.where(row < 8, low_y, jnp.where(row < 16, 1.0, high_y)) * (1.0 / 6.0)
    factors[0] = factor * exists(-1, 0).astype(F32)
    factors[1] = factor
    factors[2] = factor * exists(1, 0).astype(F32)
    summed[...] = jnp.zeros_like(summed)
    packed[...] = jnp.zeros_like(packed)

    for one in loads[0:4]:
        one.wait()
    for f in range(6):
        own = wide[f, 2:10]
        edge_send[0, f] = own[:, 6:8]
        edge_send[1, f] = own[:, 0:2]
    pl.semaphore_wait(barrier, sum(exists(dx, dy).astype(jnp.int32) for dx, dy in AROUND))
    halo = [
        copy(wide.at[:, pl.ds(8, 2)], wide.at[:, pl.ds(0, 2)], send_halo, recv_halo, 0, SIDES[0]),
        copy(wide.at[:, pl.ds(2, 2)], wide.at[:, pl.ds(10, 2)], send_halo, recv_halo, 1, SIDES[1]),
        copy(edge_send.at[0], edge_recv.at[0], send_halo, recv_halo, 2, SIDES[2]),
        copy(edge_send.at[1], edge_recv.at[1], send_halo, recv_halo, 3, SIDES[3]),
    ]
    start(halo, SIDES)

    high, low = split(wide[0:4, 2:10].reshape(4 * rows, depth))
    grid_pieces[...] = jnp.concatenate([high, low], axis=0).astype(BF16)
    for one in loads[4:]:
        one.wait()

    def exchange(turn, carry):
        here = pl.ds(pl.multiple_of(turn * CHUNK, CHUNK), CHUNK)
        cells = cell[:, here]
        goal = target[:, here]
        diameter = size[:, here]
        moving = motion[:, 0, here]
        at_z = jnp.bitwise_and(cells, depth - 1)
        at_xy = lax.shift_right_logical(cells, 8)
        hot_z = (lax.broadcasted_iota(jnp.int32, (depth, CHUNK), 0) == at_z).astype(F32).astype(BF16)
        hot_xy = (lax.broadcasted_iota(jnp.int32, (rows, CHUNK), 0) == at_xy).astype(F32)
        found = jnp.dot(grid_pieces[...], hot_z, preferred_element_type=F32)
        found = found[: 4 * rows] + found[4 * rows :]
        local = jnp.concatenate(
            [jnp.sum(found[f * rows : (f + 1) * rows] * hot_xy, axis=0, keepdims=True) for f in range(4)], axis=0
        )
        gap = local - moving
        field = lax.broadcasted_iota(jnp.int32, gap.shape, 0)
        pace = jnp.where(field == 3, TIME_STEP / HEAT_TIME, TIME_STEP / DRAG_TIME)
        fall = jnp.where(field == 2, TIME_STEP * GRAVITY, 0.0)
        carried = moving + pace * gap - fall
        vapour = VAPOUR_RATE * diameter * (1.0 / (1.0 + jnp.exp(-gap[3:4])))
        fresh = jnp.concatenate([carried, diameter - TIME_STEP * vapour], axis=0)
        renewed[0:5, here] = fresh
        kept[:, 0, here] = jnp.where(goal == 4, fresh, 0.0)
        alive = goal >= 0
        drag = jnp.where(alive, -DRAG_COUPLING * diameter * diameter * gap[2:3], 0.0)
        vapour = jnp.where(alive, vapour, 0.0)
        drag_high, drag_low = split(drag)
        vapour_high, vapour_low = split(vapour)
        spread = jnp.concatenate(
            [hot_xy * drag_high, hot_xy * vapour_high, hot_xy * drag_low, hot_xy * vapour_low], axis=0
        ).astype(BF16)
        summed[...] += lax.dot_general(spread, hot_z, NT, preferred_element_type=F32)
        return carry

    turns = slots // CHUNK
    lax.fori_loop(0, turns // 2, exchange, 0)

    receive(halo, SIDES)
    for f in range(6):
        tall[f, :, 6:8] = edge_recv[0, f]
        tall[f, :, 16:18] = edge_recv[1, f]
    for f in range(5):
        centre = wide[f, 2:10]
        near_x, near_x2 = wide[f, 3:11], wide[f, 1:9]
        near_y, near_y2 = tall[f, :, 9:17], tall[f, :, 7:15]
        near_z, near_z2 = along_depth(centre, -1), along_depth(centre, 1)
        laplace = near_x + near_x2 + near_y + near_y2 + near_z + near_z2 - 6.0 * centre
        slope_x = 8.0 * (near_x - near_x2) - (wide[f, 4:12] - wide[f, 0:8])
        slope_y = 8.0 * (near_y - near_y2) - (tall[f, :, 10:18] - tall[f, :, 6:14])
        slope_z = 8.0 * (near_z - near_z2) - (along_depth(centre, -2) - along_depth(centre, 2))
        transport = (wide[0, 2:10] * slope_x + wide[1, 2:10] * slope_y + wide[2, 2:10] * slope_z) * (1.0 / 12.0)
        star[f] = centre + TIME_STEP * (DIFFUSION * laplace - transport)
        if f == 1:
            tall_v[:, 8:16] = star[1]
            v_send[0] = star[1, :, 7:8]
            v_send[1] = star[1, :, 0:1]
            u_halo[2] = star[0, 7]
            u_halo[3] = star[0, 0]
            edges = [
                copy(u_halo.at[2], u_halo.at[0], send_star, recv_star, 0, SIDES[0]),
                copy(u_halo.at[3], u_halo.at[1], send_star, recv_star, 1, SIDES[1]),
                copy(v_send.at[0], v_recv.at[0], send_star, recv_star, 2, SIDES[2]),
                copy(v_send.at[1], v_recv.at[1], send_star, recv_star, 3, SIDES[3]),
            ]
            start(edges, SIDES)

    own = (pl.ds(8, 8), pl.ds(8, 8))
    tile_row = lax.broadcasted_iota(jnp.int32, (8, 256), 0)

    def layer(dx, i):
        return 8 - i if dx > 0 else i - 1

    def blocks(buffer, which, send, recv):
        block = buffer[own]
        for way, (dx, dy) in enumerate(CORNERS):
            for i in range(1, 5):
                near, far = block[layer(dx, i)], block[layer(dx, 9 - i)]
                if i > 1:
                    if dy > 0:
                        near = jnp.where(tile_row >= i, near, pltpu.roll(far, i - 1, 0))
                    else:
                        near = jnp.where(tile_row < 8 - i, near, pltpu.roll(far, 9 - i, 0))
                corner_send[which, way, i - 1] = near
        copies = [
            copy(
                buffer.at[own], buffer.at[pl.ds(8 - 8 * dx, 8), pl.ds(8 - 8 * dy, 8)],
                send, recv, spot, (dx, dy),
            )
            for spot, (dx, dy) in enumerate(SIDES)
        ]
        copies += [
            copy(corner_send.at[which, way], corner_recv.at[which, way], send, recv, 4 + way, side)
            for way, side in enumerate(CORNERS)
        ]
        start(copies, AROUND)
        return copies

    def unpack(buffer, which):
        for way, (dx, dy) in enumerate(CORNERS):
            base, side = 8 - 8 * dx, slice(8 - 8 * dy, 16 - 8 * dy)
            for i in range(1, 5):
                tile = corner_recv[which, way, i - 1]
                buffer[base + layer(dx, i), side] = tile
                back = (9 - i if dy > 0 else i - 1) % 8
                buffer[base + layer(dx, 9 - i), side] = pltpu.roll(tile, back, 0) if back else tile

    sums[own] = (
        wide[5, 3:11] + wide[5, 1:9] + tall[5, :, 9:17] + tall[5, :, 7:15]
        + along_depth(wide[5, 2:10], 1) + along_depth(wide[5, 2:10], -1)
    )
    sum_copies = blocks(sums, 0, send_sum, recv_sum)

    lax.fori_loop(turns // 2, turns, exchange, 0)

    numbers = lax.broadcasted_iota(jnp.int32, (rows, depth), 0) * depth + lax.broadcasted_iota(
        jnp.int32, (rows, depth), 1
    )
    ramp = jnp.clip((CLOCK - spray_time[...].astype(F32)) / SPRAY_RAMP, 0.0, 1.0)
    strength = SPRAY_RATE * ramp * spray_on[...].astype(F32)
    spray = jnp.zeros((rows, depth), F32)
    for head in range(spray_on.shape[1]):
        spray += jnp.where(numbers == spray_cell[:, head : head + 1], strength[:, head : head + 1], 0.0)
    total = summed[...]
    drag = total[:rows] + total[2 * rows : 3 * rows]
    vapour = total[rows : 2 * rows] + total[3 * rows :]
    lift = star[2] + (TIME_STEP * (drag - spray)).reshape(8, 8, 256)
    star[2] = lift

    receive(edges, SIDES)
    tall_v[:, 7:8] = v_recv[0]
    tall_v[:, 16:17] = v_recv[1]
    speed = star[0]
    spread_x = jnp.concatenate([speed[1:8], u_halo[1:2]], axis=0) - jnp.concatenate(
        [u_halo[0:1], speed[0:7]], axis=0
    )
    spread = spread_x + (tall_v[:, 9:17] - tall_v[:, 7:15]) + (along_depth(lift, -1) - along_depth(lift, 1))
    parts[own] = spread * (0.5 / TIME_STEP)
    part_copies = blocks(parts, 1, send_src, recv_src)

    star[3] = star[3] + (TIME_STEP * (-LATENT * vapour - spray)).reshape(8, 8, 256)
    star[4] = star[4] + (TIME_STEP * vapour).reshape(8, 8, 256)

    early = [
        pltpu.make_async_copy(star.at[pl.ds(3, 2)], gas_next.at[pl.ds(3, 2)], send_out.at[0]),
        pltpu.make_async_copy(kept, kept_hbm, send_out.at[1]),
    ]
    for one in early:
        one.start()

    upper = (
        lax.broadcasted_iota(jnp.int32, (256, 256), 0) <= lax.broadcasted_iota(jnp.int32, (256, 256), 1)
    ).astype(F32).astype(BF16)
    eight = lax.broadcasted_iota(jnp.int32, (8, 256), 0)

    def pack(turn, carry):
        here = pl.ds(pl.multiple_of(turn * CHUNK, CHUNK), CHUNK)
        goal = target[:, here]
        pieces = [(eight == goal[:, k * 256 : k * 256 + 256]).astype(F32) for k in range(CHUNK // 256)]
        counts = jnp.dot(jnp.concatenate(pieces, axis=0).astype(BF16), upper, preferred_element_type=F32)
        places = []
        for k, piece in enumerate(pieces):
            count = counts[8 * k : 8 * k + 8] + carry
            carry = count[:, 255:256]
            place = jnp.where(eight < 4, piece * (count + (512.0 * eight.astype(F32))), 0.0)
            places.append(jnp.sum(place, axis=0, keepdims=True))
        place = jnp.concatenate(places, axis=1).astype(jnp.int32) - 1
        hot_low = (
            lax.broadcasted_iota(jnp.int32, (256, CHUNK), 0) == jnp.bitwise_and(place, 255)
        ).astype(F32).astype(BF16)
        hot_high = (
            lax.broadcasted_iota(jnp.int32, (8, CHUNK), 0) == lax.shift_right_arithmetic(place, 8)
        ).astype(F32)
        top, rest = split(renewed[0:5, here])
        bundle = jnp.concatenate(
            [hot_high * top[f : f + 1] for f in range(5)] + [hot_high * rest[f : f + 1] for f in range(5)], axis=0
        ).astype(BF16)
        packed[...] += lax.dot_general(bundle, hot_low, NT, preferred_element_type=F32)
        return carry

    lax.fori_loop(0, turns, pack, jnp.zeros((8, 1), F32))
    bundle = packed[0:40] + packed[40:80]
    for f in range(5):
        for way in range(4):
            for half in range(2):
                spot = f * 8 + 2 * way + half
                parcels[way, f : f + 1, half * 256 : half * 256 + 256] = bundle[spot : spot + 1]
    for way in range(4):
        parcels[way, 5:8] = jnp.zeros((3, 512), F32)
    parcel = [
        copy(parcels.at[way], landed.at[way], send_parcel, recv_parcel, way, SIDES[way]) for way in range(4)
    ]
    start(parcel, SIDES)

    receive(sum_copies, AROUND)
    unpack(sums, 0)
    receive(part_copies, AROUND)
    unpack(parts, 1)

    for x in range(0, 24, 4):
        swap[0, x : x + 4] = (sums[x : x + 4] - parts[x : x + 4]) * factors[x // 8]
    for turn in range(1, ITERS):
        old, new = swap.at[(turn - 1) % 2], swap.at[turn % 2]
        x = turn
        while x < 24 - turn:
            end = min(x + 4, 24 - turn, (x // 8 + 1) * 8)
            centre = old[x:end]
            total = old[x - 1 : end - 1] + old[x + 1 : end + 1]
            total = total + pltpu.roll(centre, 1, 1) + pltpu.roll(centre, 23, 1)
            total = total + along_depth(centre, 1) + along_depth(centre, -1)
            new[x:end] = (total - parts[x:end]) * factors[x // 8]
            x = end

    last = swap.at[(ITERS - 1) % 2]
    centre = last[8:16, 8:16]
    final[...] = centre
    half = TIME_STEP * 0.5
    star[0] = star[0] - half * (last[9:17, 8:16] - last[7:15, 8:16])
    star[1] = star[1] - half * (last[8:16, 9:17] - last[8:16, 7:15])
    star[2] = star[2] - half * (along_depth(centre, -1) - along_depth(centre, 1))
    late = [
        pltpu.make_async_copy(star.at[pl.ds(0, 3)], gas_next.at[pl.ds(0, 3)], send_out.at[2]),
        pltpu.make_async_copy(final, pressure, send_out.at[3]),
    ]
    for one in late:
        one.start()
    receive(parcel, SIDES)
    for way in range(4):
        arrived[way, :, 0, :] = landed[way, 0:5]
    late.append(pltpu.make_async_copy(arrived, arrived_hbm, send_out.at[4]))
    late[2].start()

    sent(halo, SIDES)
    sent(edges, SIDES)
    sent(sum_copies, AROUND)
    sent(part_copies, AROUND)
    sent(parcel, SIDES)
    for one in early + late:
        one.wait()


def hand_over_kernel(*refs):
    sems = refs[-1]
    copies = [pltpu.make_async_copy(refs[k], refs[4 + k], sems.at[k]) for k in range(4)]
    for one in copies:
        one.start()
    for one in copies:
        one.wait()


def body(
    n_gx, n_gy,
    gas_state, pressure_guess, drop_motion, drop_size, drop_cell, drop_target, spray_on, spray_time, spray_cell,
):
    hbm = pl.BlockSpec(memory_space=pltpu.HBM)
    dma = pltpu.SemaphoreType.DMA
    slots = drop_size.shape[1]
    heads = spray_on.shape[1]
    block = gas_state.shape[1:]
    shape = functools.partial(jax.ShapeDtypeStruct, dtype=F32)
    outs = (shape(gas_state.shape), shape(block), shape((5, 1, slots)), shape((4, 5, 1, 512)))
    results = pl.pallas_call(
        functools.partial(evolve_kernel, n_gx, n_gy),
        out_shape=outs,
        in_specs=[hbm] * 9,
        out_specs=(hbm,) * 4,
        scratch_shapes=[
            pltpu.VMEM(gas_state.shape, F32),
            pltpu.VMEM((3, 24, 256), F32),
            pltpu.VMEM((5, 1, slots), F32),
            pltpu.VMEM((4, 5, 1, 512), F32),
            pltpu.VMEM((2, 24, 24, 256), F32),
            pltpu.VMEM(block, F32),
            pltpu.VMEM(drop_motion.shape, F32),
            pltpu.VMEM((1, slots), F32),
            pltpu.VMEM((1, slots), jnp.int32),
            pltpu.VMEM((1, slots), jnp.int32),
            pltpu.VMEM((1, heads), jnp.int32),
            pltpu.VMEM((1, heads), jnp.int32),
            pltpu.VMEM((1, heads), jnp.int32),
            pltpu.VMEM((512, 256), BF16),
            pltpu.VMEM((256, 256), F32),
            pltpu.VMEM((80, 256), F32),
            pltpu.VMEM((8, slots), F32),
            pltpu.VMEM((4, 8, 512), F32),
            pltpu.VMEM((4, 8, 512), F32),
            pltpu.VMEM((6, 12, 8, 256), F32),
            pltpu.VMEM((6, 8, 24, 256), F32),
            pltpu.VMEM((2, 6, 8, 2, 256), F32),
            pltpu.VMEM((2, 6, 8, 2, 256), F32),
            pltpu.VMEM((24, 24, 256), F32),
            pltpu.VMEM((24, 24, 256), F32),
            pltpu.VMEM((2, 4, 4, 8, 256), F32),
            pltpu.VMEM((2, 4, 4, 8, 256), F32),
            pltpu.VMEM((8, 24, 256), F32),
            pltpu.VMEM((4, 8, 256), F32),
            pltpu.VMEM((2, 8, 1, 256), F32),
            pltpu.VMEM((2, 8, 1, 256), F32),
        ]
        + [dma((11,)), dma((5,))] + [dma((4,))] * 6 + [dma((8,))] * 4,
        compiler_params=pltpu.CompilerParams(
            collective_id=0, has_side_effects=True, vmem_limit_bytes=60 * 1024 * 1024
        ),
    )(
        gas_state, pressure_guess, drop_motion, drop_size, drop_cell, drop_target, spray_on, spray_time, spray_cell
    )
    return pl.pallas_call(
        hand_over_kernel,
        out_shape=outs,
        in_specs=[hbm] * 4,
        out_specs=(hbm,) * 4,
        scratch_shapes=[dma((4,))],
        compiler_params=pltpu.CompilerParams(vmem_limit_bytes=60 * 1024 * 1024),
    )(*results)


def solution(mesh):
    in_specs = (
        P(None, "gx", "gy", None),
        P("gx", "gy", None),
        P(None, "gx", "gy"),
    ) + (P("gx", "gy"),) * 6
    out_specs = (
        P(None, "gx", "gy", None),
        P("gx", "gy", None),
        P(None, "gx", "gy"),
        P(None, None, "gx", "gy"),
    )
    inner = functools.partial(body, mesh.shape["gx"], mesh.shape["gy"])
    return jax.shard_map(inner, mesh=mesh, in_specs=in_specs, out_specs=out_specs, check_vma=False)
```

```python
import functools

import jax
import jax.numpy as jnp
from jax import lax
from jax.experimental import pallas as pl
from jax.experimental.pallas import tpu as pltpu
from jax.sharding import PartitionSpec as P

ITERS = 8
TIME_STEP = 0.2
DIFFUSION = 0.1
DRAG_TIME = 0.5
HEAT_TIME = 1.0
GRAVITY = 1.0
VAPOUR_RATE = 0.5
DRAG_COUPLING = 0.5
LATENT = 2.0
SPRAY_RATE = 3.0
CLOCK = 100.0
SPRAY_RAMP = 50.0

MESH = pl.DeviceIdType.MESH
F32 = jnp.float32
BF16 = jnp.bfloat16
CHUNK = 1024
NT = (((1,), (1,)), ((), ()))
SIDES = ((1, 0), (-1, 0), (0, 1), (0, -1))
CORNERS = ((1, 1), (1, -1), (-1, 1), (-1, -1))
AROUND = SIDES + CORNERS


def split(values):
    high = values.astype(BF16).astype(F32)
    return high, values - high


def along_depth(values, by):
    lane = lax.broadcasted_iota(jnp.int32, (1, 1, 128), 2)
    first = pltpu.roll(values[:, :, :128], by % 128, 2)
    second = pltpu.roll(values[:, :, 128:], by % 128, 2)
    if by > 0:
        return jnp.concatenate(
            [jnp.where(lane < by, 0.0, first), jnp.where(lane < by, first, second)], axis=2
        )
    inside = lane < 128 + by
    return jnp.concatenate([jnp.where(inside, first, second), jnp.where(inside, second, 0.0)], axis=2)


def evolve_kernel(
    n_gx, n_gy,
    gas_hbm, guess_hbm, motion_hbm, size_hbm, cell_hbm, target_hbm, on_hbm, time_hbm, place_hbm,
    gas_next, pressure, kept_hbm, arrived_hbm,
    star, factors, kept, arrived, swap, final,
    motion, size, cell, target, spray_on, spray_time, spray_cell,
    grid_pieces, summed, packed, renewed, parcels, landed,
    guess, rim, side_send, side_recv, wide, tall, edge_send, edge_recv, sums, parts, corner_send, corner_recv, tall_v, u_halo, v_send, v_recv,
    send_in, send_out, send_rim, recv_rim, send_halo, recv_halo, send_star, recv_star, send_parcel, recv_parcel, send_sum, recv_sum, send_src,
    recv_src,
):
    me_x, me_y = lax.axis_index("gx"), lax.axis_index("gy")
    slots = size.shape[1]
    rows, depth = 64, 256

    def exists(dx, dy):
        to_x, to_y = me_x + dx, me_y + dy
        return (to_x >= 0) & (to_x < n_gx) & (to_y >= 0) & (to_y < n_gy)

    def device(dx, dy):
        return {"gx": jnp.clip(me_x + dx, 0, n_gx - 1), "gy": jnp.clip(me_y + dy, 0, n_gy - 1)}

    def copy(src, dst, send, recv, spot, side):
        return pltpu.make_async_remote_copy(
            src_ref=src, dst_ref=dst, send_sem=send.at[spot], recv_sem=recv.at[spot],
            device_id=device(*side), device_id_type=MESH,
        )

    def start(copies, sides):
        for one, (dx, dy) in zip(copies, sides):
            pl.when(exists(dx, dy))(one.start)

    def receive(copies, sides):
        for one, (dx, dy) in zip(copies, sides):
            pl.when(exists(-dx, -dy))(one.wait_recv)

    def sent(copies, sides):
        for one, (dx, dy) in zip(copies, sides):
            pl.when(exists(dx, dy))(one.wait_send)

    loads = [
        pltpu.make_async_copy(src, dst, send_in.at[spot])
        for spot, (src, dst) in enumerate(
            (
                (guess_hbm, rim.at[pl.ds(1, 8)]),
                (guess_hbm, guess.at[:, pl.ds(8, 8)]),
                (gas_hbm, wide.at[:, pl.ds(2, 8)]),
                (gas_hbm, tall.at[:, :, pl.ds(8, 8)]),
                (cell_hbm, cell),
                (motion_hbm, motion),
                (size_hbm, size),
                (target_hbm, target),
                (on_hbm, spray_on),
                (time_hbm, spray_time),
                (place_hbm, spray_cell),
            )
        )
    ]
    for one in loads:
        one.start()

    barrier = pltpu.get_barrier_semaphore()
    for dx, dy in AROUND:
        @pl.when(exists(dx, dy))
        def _():
            pl.semaphore_signal(barrier, inc=1, device_id=device(dx, dy), device_id_type=MESH)

    @pl.when(~exists(-1, 0))
    def _():
        wide[:, 0:2] = jnp.zeros((5, 2, 8, 256), F32)
        rim[0] = jnp.zeros((8, 256), F32)
        u_halo[0] = jnp.zeros((8, 256), F32)

    @pl.when(~exists(1, 0))
    def _():
        wide[:, 10:12] = jnp.zeros((5, 2, 8, 256), F32)
        rim[9] = jnp.zeros((8, 256), F32)
        u_halo[1] = jnp.zeros((8, 256), F32)

    @pl.when(~exists(0, -1))
    def _():
        edge_recv[0] = jnp.zeros((5, 8, 2, 256), F32)
        side_recv[0] = jnp.zeros((8, 1, 256), F32)
        v_recv[0] = jnp.zeros((8, 1, 256), F32)

    @pl.when(~exists(0, 1))
    def _():
        edge_recv[1] = jnp.zeros((5, 8, 2, 256), F32)
        side_recv[1] = jnp.zeros((8, 1, 256), F32)
        v_recv[1] = jnp.zeros((8, 1, 256), F32)

    for way, (dx, dy) in enumerate(SIDES):
        @pl.when(~exists(-dx, -dy))
        def _():
            spot = (pl.ds(8 - 8 * dx, 8), pl.ds(8 - 8 * dy, 8))
            landed[way] = jnp.zeros((8, 512), F32)
            sums[spot] = jnp.zeros((8, 8, 256), F32)
            parts[spot] = jnp.zeros((8, 8, 256), F32)

    for way, (dx, dy) in enumerate(CORNERS):
        @pl.when(~exists(-dx, -dy))
        def _():
            corner_recv[0, way] = jnp.zeros((4, 8, 256), F32)
            corner_recv[1, way] = jnp.zeros((4, 8, 256), F32)

    row = lax.broadcasted_iota(jnp.int32, (24, 256), 0)
    low_y, high_y = exists(0, -1).astype(F32), exists(0, 1).astype(F32)
    factor = jnp.where(row < 8, low_y, jnp.where(row < 16, 1.0, high_y)) * (1.0 / 6.0)
    factors[0] = factor * exists(-1, 0).astype(F32)
    factors[1] = factor
    factors[2] = factor * exists(1, 0).astype(F32)
    summed[...] = jnp.zeros_like(summed)
    packed[...] = jnp.zeros_like(packed)

    for one in loads[0:4]:
        one.wait()
    side_send[0] = rim[1:9, 7:8]
    side_send[1] = rim[1:9, 0:1]
    for f in range(5):
        own = wide[f, 2:10]
        edge_send[0, f] = own[:, 6:8]
        edge_send[1, f] = own[:, 0:2]
    pl.semaphore_wait(barrier, sum(exists(dx, dy).astype(jnp.int32) for dx, dy in AROUND))
    border = [
        copy(rim.at[8], rim.at[0], send_rim, recv_rim, 0, SIDES[0]),
        copy(rim.at[1], rim.at[9], send_rim, recv_rim, 1, SIDES[1]),
        copy(side_send.at[0], side_recv.at[0], send_rim, recv_rim, 2, SIDES[2]),
        copy(side_send.at[1], side_recv.at[1], send_rim, recv_rim, 3, SIDES[3]),
    ]
    start(border, SIDES)
    halo = [
        copy(wide.at[:, pl.ds(8, 2)], wide.at[:, pl.ds(0, 2)], send_halo, recv_halo, 0, SIDES[0]),
        copy(wide.at[:, pl.ds(2, 2)], wide.at[:, pl.ds(10, 2)], send_halo, recv_halo, 1, SIDES[1]),
        copy(edge_send.at[0], edge_recv.at[0], send_halo, recv_halo, 2, SIDES[2]),
        copy(edge_send.at[1], edge_recv.at[1], send_halo, recv_halo, 3, SIDES[3]),
    ]
    start(halo, SIDES)

    high, low = split(wide[0:4, 2:10].reshape(4 * rows, depth))
    grid_pieces[...] = jnp.concatenate([high, low], axis=0).astype(BF16)
    for one in loads[4:]:
        one.wait()

    def exchange(turn):
        here = slice(turn * CHUNK, turn * CHUNK + CHUNK)
        cells = cell[:, here]
        goal = target[:, here]
        diameter = size[:, here]
        moving = motion[:, 0, here]
        at_z = jnp.bitwise_and(cells, depth - 1)
        at_xy = lax.shift_right_logical(cells, 8)
        hot_z = (lax.broadcasted_iota(jnp.int32, (depth, CHUNK), 0) == at_z).astype(F32).astype(BF16)
        hot_xy = (lax.broadcasted_iota(jnp.int32, (rows, CHUNK), 0) == at_xy).astype(F32)
        found = jnp.dot(grid_pieces[...], hot_z, preferred_element_type=F32)
        found = found[: 4 * rows] + found[4 * rows :]
        local = jnp.concatenate(
            [jnp.sum(found[f * rows : (f + 1) * rows] * hot_xy, axis=0, keepdims=True) for f in range(4)], axis=0
        )
        gap = local - moving
        field = lax.broadcasted_iota(jnp.int32, gap.shape, 0)
        pace = jnp.where(field == 3, TIME_STEP / HEAT_TIME, TIME_STEP / DRAG_TIME)
        fall = jnp.where(field == 2, TIME_STEP * GRAVITY, 0.0)
        carried = moving + pace * gap - fall
        vapour = VAPOUR_RATE * diameter * (1.0 / (1.0 + jnp.exp(-gap[3:4])))
        fresh = jnp.concatenate([carried, diameter - TIME_STEP * vapour], axis=0)
        renewed[0:5, here] = fresh
        kept[:, 0, here] = jnp.where(goal == 4, fresh, 0.0)
        alive = goal >= 0
        drag = jnp.where(alive, -DRAG_COUPLING * diameter * diameter * gap[2:3], 0.0)
        vapour = jnp.where(alive, vapour, 0.0)
        drag_high, drag_low = split(drag)
        vapour_high, vapour_low = split(vapour)
        spread = jnp.concatenate(
            [hot_xy * drag_high, hot_xy * vapour_high, hot_xy * drag_low, hot_xy * vapour_low], axis=0
        ).astype(BF16)
        summed[...] += lax.dot_general(spread, hot_z, NT, preferred_element_type=F32)

    turns = slots // CHUNK
    exchange(0)

    own = (pl.ds(8, 8), pl.ds(8, 8))
    tile_row = lax.broadcasted_iota(jnp.int32, (8, 256), 0)

    def layer(dx, i):
        return 8 - i if dx > 0 else i - 1

    def blocks(buffer, which, send, recv):
        block = buffer[own]
        for way, (dx, dy) in enumerate(CORNERS):
            for i in range(1, 5):
                near, far = block[layer(dx, i)], block[layer(dx, 9 - i)]
                if i > 1:
                    if dy > 0:
                        near = jnp.where(tile_row >= i, near, pltpu.roll(far, i - 1, 0))
                    else:
                        near = jnp.where(tile_row < 8 - i, near, pltpu.roll(far, 9 - i, 0))
                corner_send[which, way, i - 1] = near
        copies = [
            copy(
                buffer.at[own], buffer.at[pl.ds(8 - 8 * dx, 8), pl.ds(8 - 8 * dy, 8)],
                send, recv, spot, (dx, dy),
            )
            for spot, (dx, dy) in enumerate(SIDES)
        ]
        copies += [
            copy(corner_send.at[which, way], corner_recv.at[which, way], send, recv, 4 + way, side)
            for way, side in enumerate(CORNERS)
        ]
        start(copies, AROUND)
        return copies

    def unpack(buffer, which):
        for way, (dx, dy) in enumerate(CORNERS):
            base, side = 8 - 8 * dx, slice(8 - 8 * dy, 16 - 8 * dy)
            for i in range(1, 5):
                tile = corner_recv[which, way, i - 1]
                buffer[base + layer(dx, i), side] = tile
                back = (9 - i if dy > 0 else i - 1) % 8
                buffer[base + layer(dx, 9 - i), side] = pltpu.roll(tile, back, 0) if back else tile

    receive(border, SIDES)
    guess[:, 7:8] = side_recv[0]
    guess[:, 16:17] = side_recv[1]
    sums[own] = (
        rim[2:10] + rim[0:8] + guess[:, 9:17] + guess[:, 7:15]
        + along_depth(rim[1:9], 1) + along_depth(rim[1:9], -1)
    )
    sum_copies = blocks(sums, 0, send_sum, recv_sum)

    for turn in range(1, turns - 1):
        exchange(turn)

    receive(halo, SIDES)
    for f in range(5):
        tall[f, :, 6:8] = edge_recv[0, f]
        tall[f, :, 16:18] = edge_recv[1, f]
    for f in range(5):
        centre = wide[f, 2:10]
        near_x, near_x2 = wide[f, 3:11], wide[f, 1:9]
        near_y, near_y2 = tall[f, :, 9:17], tall[f, :, 7:15]
        near_z, near_z2 = along_depth(centre, -1), along_depth(centre, 1)
        laplace = near_x + near_x2 + near_y + near_y2 + near_z + near_z2 - 6.0 * centre
        slope_x = 8.0 * (near_x - near_x2) - (wide[f, 4:12] - wide[f, 0:8])
        slope_y = 8.0 * (near_y - near_y2) - (tall[f, :, 10:18] - tall[f, :, 6:14])
        slope_z = 8.0 * (near_z - near_z2) - (along_depth(centre, -2) - along_depth(centre, 2))
        transport = (wide[0, 2:10] * slope_x + wide[1, 2:10] * slope_y + wide[2, 2:10] * slope_z) * (1.0 / 12.0)
        star[f] = centre + TIME_STEP * (DIFFUSION * laplace - transport)
        if f == 1:
            tall_v[:, 8:16] = star[1]
            v_send[0] = star[1, :, 7:8]
            v_send[1] = star[1, :, 0:1]
            u_halo[2] = star[0, 7]
            u_halo[3] = star[0, 0]
            edges = [
                copy(u_halo.at[2], u_halo.at[0], send_star, recv_star, 0, SIDES[0]),
                copy(u_halo.at[3], u_halo.at[1], send_star, recv_star, 1, SIDES[1]),
                copy(v_send.at[0], v_recv.at[0], send_star, recv_star, 2, SIDES[2]),
                copy(v_send.at[1], v_recv.at[1], send_star, recv_star, 3, SIDES[3]),
            ]
            start(edges, SIDES)

    exchange(turns - 1)

    numbers = lax.broadcasted_iota(jnp.int32, (rows, depth), 0) * depth + lax.broadcasted_iota(
        jnp.int32, (rows, depth), 1
    )
    ramp = jnp.clip((CLOCK - spray_time[...].astype(F32)) / SPRAY_RAMP, 0.0, 1.0)
    strength = SPRAY_RATE * ramp * spray_on[...].astype(F32)
    spray = jnp.zeros((rows, depth), F32)
    for head in range(spray_on.shape[1]):
        spray += jnp.where(numbers == spray_cell[:, head : head + 1], strength[:, head : head + 1], 0.0)
    total = summed[...]
    drag = total[:rows] + total[2 * rows : 3 * rows]
    vapour = total[rows : 2 * rows] + total[3 * rows :]
    lift = star[2] + (TIME_STEP * (drag - spray)).reshape(8, 8, 256)
    star[2] = lift

    receive(edges, SIDES)
    tall_v[:, 7:8] = v_recv[0]
    tall_v[:, 16:17] = v_recv[1]
    speed = star[0]
    spread_x = jnp.concatenate([speed[1:8], u_halo[1:2]], axis=0) - jnp.concatenate(
        [u_halo[0:1], speed[0:7]], axis=0
    )
    spread = spread_x + (tall_v[:, 9:17] - tall_v[:, 7:15]) + (along_depth(lift, -1) - along_depth(lift, 1))
    parts[own] = spread * (0.5 / TIME_STEP)
    part_copies = blocks(parts, 1, send_src, recv_src)

    star[3] = star[3] + (TIME_STEP * (-LATENT * vapour - spray)).reshape(8, 8, 256)
    star[4] = star[4] + (TIME_STEP * vapour).reshape(8, 8, 256)

    early = [
        pltpu.make_async_copy(star.at[pl.ds(3, 2)], gas_next.at[pl.ds(3, 2)], send_out.at[0]),
        pltpu.make_async_copy(kept, kept_hbm, send_out.at[1]),
    ]
    for one in early:
        one.start()

    upper = (
        lax.broadcasted_iota(jnp.int32, (256, 256), 0) <= lax.broadcasted_iota(jnp.int32, (256, 256), 1)
    ).astype(F32).astype(BF16)
    eight = lax.broadcasted_iota(jnp.int32, (8, 256), 0)

    def pack(turn, carry):
        here = pl.ds(pl.multiple_of(turn * CHUNK, CHUNK), CHUNK)
        goal = target[:, here]
        pieces = [(eight == goal[:, k * 256 : k * 256 + 256]).astype(F32) for k in range(CHUNK // 256)]
        counts = jnp.dot(jnp.concatenate(pieces, axis=0).astype(BF16), upper, preferred_element_type=F32)
        places = []
        for k, piece in enumerate(pieces):
            count = counts[8 * k : 8 * k + 8] + carry
            carry = count[:, 255:256]
            place = jnp.where(eight < 4, piece * (count + (512.0 * eight.astype(F32))), 0.0)
            places.append(jnp.sum(place, axis=0, keepdims=True))
        place = jnp.concatenate(places, axis=1).astype(jnp.int32) - 1
        hot_low = (
            lax.broadcasted_iota(jnp.int32, (256, CHUNK), 0) == jnp.bitwise_and(place, 255)
        ).astype(F32).astype(BF16)
        hot_high = (
            lax.broadcasted_iota(jnp.int32, (8, CHUNK), 0) == lax.shift_right_arithmetic(place, 8)
        ).astype(F32)
        top, rest = split(renewed[0:5, here])
        bundle = jnp.concatenate(
            [hot_high * top[f : f + 1] for f in range(5)] + [hot_high * rest[f : f + 1] for f in range(5)], axis=0
        ).astype(BF16)
        packed[...] += lax.dot_general(bundle, hot_low, NT, preferred_element_type=F32)
        return carry

    lax.fori_loop(0, turns, pack, jnp.zeros((8, 1), F32))
    bundle = packed[0:40] + packed[40:80]
    for f in range(5):
        for way in range(4):
            for half in range(2):
                spot = f * 8 + 2 * way + half
                parcels[way, f : f + 1, half * 256 : half * 256 + 256] = bundle[spot : spot + 1]
    for way in range(4):
        parcels[way, 5:8] = jnp.zeros((3, 512), F32)
    parcel = [
        copy(parcels.at[way], landed.at[way], send_parcel, recv_parcel, way, SIDES[way]) for way in range(4)
    ]
    start(parcel, SIDES)

    receive(sum_copies, AROUND)
    unpack(sums, 0)
    receive(part_copies, AROUND)
    unpack(parts, 1)

    for x in range(0, 24, 4):
        swap[0, x : x + 4] = (sums[x : x + 4] - parts[x : x + 4]) * factors[x // 8]
    for turn in range(1, ITERS):
        old, new = swap.at[(turn - 1) % 2], swap.at[turn % 2]
        x = turn
        while x < 24 - turn:
            end = min(x + 4, 24 - turn, (x // 8 + 1) * 8)
            centre = old[x:end]
            total = old[x - 1 : end - 1] + old[x + 1 : end + 1]
            total = total + pltpu.roll(centre, 1, 1) + pltpu.roll(centre, 23, 1)
            total = total + along_depth(centre, 1) + along_depth(centre, -1)
            new[x:end] = (total - parts[x:end]) * factors[x // 8]
            x = end

    last = swap.at[(ITERS - 1) % 2]
    centre = last[8:16, 8:16]
    final[...] = centre
    half = TIME_STEP * 0.5
    star[0] = star[0] - half * (last[9:17, 8:16] - last[7:15, 8:16])
    star[1] = star[1] - half * (last[8:16, 9:17] - last[8:16, 7:15])
    star[2] = star[2] - half * (along_depth(centre, -1) - along_depth(centre, 1))
    late = [
        pltpu.make_async_copy(star.at[pl.ds(0, 3)], gas_next.at[pl.ds(0, 3)], send_out.at[2]),
        pltpu.make_async_copy(final, pressure, send_out.at[3]),
    ]
    for one in late:
        one.start()
    receive(parcel, SIDES)
    for way in range(4):
        arrived[way, :, 0, :] = landed[way, 0:5]
    late.append(pltpu.make_async_copy(arrived, arrived_hbm, send_out.at[4]))
    late[2].start()

    sent(border, SIDES)
    sent(halo, SIDES)
    sent(edges, SIDES)
    sent(sum_copies, AROUND)
    sent(part_copies, AROUND)
    sent(parcel, SIDES)
    for one in early + late:
        one.wait()


def hand_over_kernel(*refs):
    sems = refs[-1]
    into = [pltpu.make_async_copy(refs[k], refs[8 + k], sems.at[k]) for k in range(4)]
    out = [pltpu.make_async_copy(refs[8 + k], refs[4 + k], sems.at[4 + k]) for k in range(4)]
    for one in into:
        one.start()
    for k in (3, 1, 2, 0):
        into[k].wait()
        out[k].start()
    for one in out:
        one.wait()


def body(
    n_gx, n_gy,
    gas_state, pressure_guess, drop_motion, drop_size, drop_cell, drop_target, spray_on, spray_time, spray_cell,
):
    hbm = pl.BlockSpec(memory_space=pltpu.HBM)
    dma = pltpu.SemaphoreType.DMA
    slots = drop_size.shape[1]
    heads = spray_on.shape[1]
    block = gas_state.shape[1:]
    shape = functools.partial(jax.ShapeDtypeStruct, dtype=F32)
    outs = (shape(gas_state.shape), shape(block), shape((5, 1, slots)), shape((4, 5, 1, 512)))
    results = pl.pallas_call(
        functools.partial(evolve_kernel, n_gx, n_gy),
        out_shape=outs,
        in_specs=[hbm] * 9,
        out_specs=(hbm,) * 4,
        scratch_shapes=[
            pltpu.VMEM(gas_state.shape, F32),
            pltpu.VMEM((3, 24, 256), F32),
            pltpu.VMEM((5, 1, slots), F32),
            pltpu.VMEM((4, 5, 1, 512), F32),
            pltpu.VMEM((2, 24, 24, 256), F32),
            pltpu.VMEM(block, F32),
            pltpu.VMEM(drop_motion.shape, F32),
            pltpu.VMEM((1, slots), F32),
            pltpu.VMEM((1, slots), jnp.int32),
            pltpu.VMEM((1, slots), jnp.int32),
            pltpu.VMEM((1, heads), jnp.int32),
            pltpu.VMEM((1, heads), jnp.int32),
            pltpu.VMEM((1, heads), jnp.int32),
            pltpu.VMEM((512, 256), BF16),
            pltpu.VMEM((256, 256), F32),
            pltpu.VMEM((80, 256), F32),
            pltpu.VMEM((8, slots), F32),
            pltpu.VMEM((4, 8, 512), F32),
            pltpu.VMEM((4, 8, 512), F32),
            pltpu.VMEM((8, 24, 256), F32),
            pltpu.VMEM((10, 8, 256), F32),
            pltpu.VMEM((2, 8, 1, 256), F32),
            pltpu.VMEM((2, 8, 1, 256), F32),
            pltpu.VMEM((5, 12, 8, 256), F32),
            pltpu.VMEM((5, 8, 24, 256), F32),
            pltpu.VMEM((2, 5, 8, 2, 256), F32),
            pltpu.VMEM((2, 5, 8, 2, 256), F32),
            pltpu.VMEM((24, 24, 256), F32),
            pltpu.VMEM((24, 24, 256), F32),
            pltpu.VMEM((2, 4, 4, 8, 256), F32),
            pltpu.VMEM((2, 4, 4, 8, 256), F32),
            pltpu.VMEM((8, 24, 256), F32),
            pltpu.VMEM((4, 8, 256), F32),
            pltpu.VMEM((2, 8, 1, 256), F32),
            pltpu.VMEM((2, 8, 1, 256), F32),
        ]
        + [dma((11,)), dma((5,))] + [dma((4,))] * 8 + [dma((8,))] * 4,
        compiler_params=pltpu.CompilerParams(
            collective_id=0, has_side_effects=True, vmem_limit_bytes=60 * 1024 * 1024
        ),
    )(
        gas_state, pressure_guess, drop_motion, drop_size, drop_cell, drop_target, spray_on, spray_time, spray_cell
    )
    return pl.pallas_call(
        hand_over_kernel,
        out_shape=outs,
        in_specs=[hbm] * 4,
        out_specs=(hbm,) * 4,
        scratch_shapes=[pltpu.VMEM(one.shape, F32) for one in outs] + [dma((8,))],
        compiler_params=pltpu.CompilerParams(vmem_limit_bytes=60 * 1024 * 1024),
    )(*results)


def solution(mesh):
    in_specs = (
        P(None, "gx", "gy", None),
        P("gx", "gy", None),
        P(None, "gx", "gy"),
    ) + (P("gx", "gy"),) * 6
    out_specs = (
        P(None, "gx", "gy", None),
        P("gx", "gy", None),
        P(None, "gx", "gy"),
        P(None, None, "gx", "gy"),
    )
    inner = functools.partial(body, mesh.shape["gx"], mesh.shape["gy"])
    return jax.shard_map(inner, mesh=mesh, in_specs=in_specs, out_specs=out_specs, check_vma=False)
```

```python
import functools

import jax
import jax.numpy as jnp
from jax import lax
from jax.experimental import pallas as pl
from jax.experimental.pallas import tpu as pltpu
from jax.sharding import PartitionSpec as P

ITERS = 8
TIME_STEP = 0.2
DIFFUSION = 0.1
DRAG_TIME = 0.5
HEAT_TIME = 1.0
GRAVITY = 1.0
VAPOUR_RATE = 0.5
DRAG_COUPLING = 0.5
LATENT = 2.0
SPRAY_RATE = 3.0
CLOCK = 100.0
SPRAY_RAMP = 50.0

MESH = pl.DeviceIdType.MESH
F32 = jnp.float32
BF16 = jnp.bfloat16
CHUNK = 1024
NT = (((1,), (1,)), ((), ()))
SIDES = ((1, 0), (-1, 0), (0, 1), (0, -1))
CORNERS = ((1, 1), (1, -1), (-1, 1), (-1, -1))
AROUND = SIDES + CORNERS


def split(values):
    high = values.astype(BF16).astype(F32)
    return high, values - high


def along_depth(values, by):
    lane = lax.broadcasted_iota(jnp.int32, (1, 1, 128), 2)
    first = pltpu.roll(values[:, :, :128], by % 128, 2)
    second = pltpu.roll(values[:, :, 128:], by % 128, 2)
    if by > 0:
        return jnp.concatenate(
            [jnp.where(lane < by, 0.0, first), jnp.where(lane < by, first, second)], axis=2
        )
    inside = lane < 128 + by
    return jnp.concatenate([jnp.where(inside, first, second), jnp.where(inside, second, 0.0)], axis=2)


def along_rows(values, by):
    row = lax.broadcasted_iota(jnp.int32, (1, 8, 256), 1)
    edge = row == (0 if by > 0 else 7)
    tiles = [pltpu.roll(values[:, k : k + 8], by % 8, 1) for k in range(0, values.shape[1], 8)]
    beside = [0.0] + tiles[:-1] if by > 0 else tiles[1:] + [0.0]
    return jnp.concatenate([jnp.where(edge, other, tile) for tile, other in zip(tiles, beside)], axis=1)


def evolve_kernel(
    n_gx, n_gy,
    gas_hbm, guess_hbm, motion_hbm, size_hbm, cell_hbm, target_hbm, on_hbm, time_hbm, place_hbm,
    gas_next, pressure, kept_hbm, arrived_hbm,
    star, kept, arrived, swap, final,
    motion, size, cell, target, spray_on, spray_time, spray_cell,
    grid_pieces, summed, packed, renewed, parcels, landed,
    guess, rim, side_send, side_recv, wide, tall, edge_send, edge_recv, sums, parts, corner_send, corner_recv, tall_v, u_halo, v_send, v_recv,
    send_in, send_out, send_rim, recv_rim, send_halo, recv_halo, send_star, recv_star, send_parcel, recv_parcel, send_sum, recv_sum, send_src,
    recv_src,
):
    me_x, me_y = lax.axis_index("gx"), lax.axis_index("gy")
    slots = size.shape[1]
    rows, depth = 64, 256
    pair = n_gy == 2
    tall_rows = sums.shape[1]
    own_y = pl.multiple_of(me_y * 8, 8) if pair else 8
    own = (pl.ds(8, 8), pl.ds(own_y, 8))

    def there(dy):
        return pl.ds(own_y, 8) if pair else pl.ds(8 - 8 * dy, 8)

    def here_from(dy):
        if pair:
            return pl.ds(own_y if dy == 0 else pl.multiple_of((1 - me_y) * 8, 8), 8)
        return pl.ds(8 - 8 * dy, 8)

    def exists(dx, dy):
        to_x, to_y = me_x + dx, me_y + dy
        return (to_x >= 0) & (to_x < n_gx) & (to_y >= 0) & (to_y < n_gy)

    def device(dx, dy):
        return {"gx": jnp.clip(me_x + dx, 0, n_gx - 1), "gy": jnp.clip(me_y + dy, 0, n_gy - 1)}

    def copy(src, dst, send, recv, spot, side):
        return pltpu.make_async_remote_copy(
            src_ref=src, dst_ref=dst, send_sem=send.at[spot], recv_sem=recv.at[spot],
            device_id=device(*side), device_id_type=MESH,
        )

    def start(copies, sides):
        for one, (dx, dy) in zip(copies, sides):
            pl.when(exists(dx, dy))(one.start)

    def receive(copies, sides):
        for one, (dx, dy) in zip(copies, sides):
            pl.when(exists(-dx, -dy))(one.wait_recv)

    def sent(copies, sides):
        for one, (dx, dy) in zip(copies, sides):
            pl.when(exists(dx, dy))(one.wait_send)

    loads = [
        pltpu.make_async_copy(src, dst, send_in.at[spot])
        for spot, (src, dst) in enumerate(
            (
                (guess_hbm, rim.at[pl.ds(1, 8)]),
                (guess_hbm, guess.at[:, pl.ds(8, 8)]),
                (gas_hbm, wide.at[:, pl.ds(2, 8)]),
                (gas_hbm, tall.at[:, :, pl.ds(8, 8)]),
                (cell_hbm, cell),
                (motion_hbm, motion),
                (size_hbm, size),
                (target_hbm, target),
                (on_hbm, spray_on),
                (time_hbm, spray_time),
                (place_hbm, spray_cell),
            )
        )
    ]
    for one in loads:
        one.start()

    barrier = pltpu.get_barrier_semaphore()
    for dx, dy in AROUND:
        @pl.when(exists(dx, dy))
        def _():
            pl.semaphore_signal(barrier, inc=1, device_id=device(dx, dy), device_id_type=MESH)

    @pl.when(~exists(-1, 0))
    def _():
        wide[:, 0:2] = jnp.zeros((5, 2, 8, 256), F32)
        rim[0] = jnp.zeros((8, 256), F32)
        u_halo[0] = jnp.zeros((8, 256), F32)

    @pl.when(~exists(1, 0))
    def _():
        wide[:, 10:12] = jnp.zeros((5, 2, 8, 256), F32)
        rim[9] = jnp.zeros((8, 256), F32)
        u_halo[1] = jnp.zeros((8, 256), F32)

    @pl.when(~exists(0, -1))
    def _():
        edge_recv[0] = jnp.zeros((5, 8, 2, 256), F32)
        side_recv[0] = jnp.zeros((8, 1, 256), F32)
        v_recv[0] = jnp.zeros((8, 1, 256), F32)

    @pl.when(~exists(0, 1))
    def _():
        edge_recv[1] = jnp.zeros((5, 8, 2, 256), F32)
        side_recv[1] = jnp.zeros((8, 1, 256), F32)
        v_recv[1] = jnp.zeros((8, 1, 256), F32)

    for way, (dx, dy) in enumerate(SIDES):
        @pl.when(~exists(-dx, -dy))
        def _():
            landed[way] = jnp.zeros((8, 512), F32)
            if dy == 0 or not pair:
                spot = (pl.ds(8 - 8 * dx, 8), here_from(dy))
                sums[spot] = jnp.zeros((8, 8, 256), F32)
                parts[spot] = jnp.zeros((8, 8, 256), F32)

    for way, (dx, dy) in enumerate(CORNERS):
        @pl.when(~exists(-dx, -dy))
        def _():
            corner_recv[0, way] = jnp.zeros((4, 8, 256), F32)
            corner_recv[1, way] = jnp.zeros((4, 8, 256), F32)

    low_x, high_x = exists(-1, 0).astype(F32), exists(1, 0).astype(F32)
    if pair:
        factors = [low_x * (1.0 / 6.0), 1.0 / 6.0, high_x * (1.0 / 6.0)]
    else:
        row = lax.broadcasted_iota(jnp.int32, (1, tall_rows, 256), 1)
        low_y, high_y = exists(0, -1).astype(F32), exists(0, 1).astype(F32)
        factor = jnp.where(row < 8, low_y, jnp.where(row < 16, 1.0, high_y)) * (1.0 / 6.0)
        factors = [factor * low_x, factor, factor * high_x]
    summed[...] = jnp.zeros_like(summed)
    packed[...] = jnp.zeros_like(packed)

    for one in loads[0:4]:
        one.wait()
    side_send[0] = rim[1:9, 7:8]
    side_send[1] = rim[1:9, 0:1]
    for f in range(5):
        inner = wide[f, 2:10]
        edge_send[0, f] = inner[:, 6:8]
        edge_send[1, f] = inner[:, 0:2]
    pl.semaphore_wait(barrier, sum(exists(dx, dy).astype(jnp.int32) for dx, dy in AROUND))
    border = [
        copy(rim.at[8], rim.at[0], send_rim, recv_rim, 0, SIDES[0]),
        copy(rim.at[1], rim.at[9], send_rim, recv_rim, 1, SIDES[1]),
        copy(side_send.at[0], side_recv.at[0], send_rim, recv_rim, 2, SIDES[2]),
        copy(side_send.at[1], side_recv.at[1], send_rim, recv_rim, 3, SIDES[3]),
    ]
    start(border, SIDES)
    halo = [
        copy(wide.at[:, pl.ds(8, 2)], wide.at[:, pl.ds(0, 2)], send_halo, recv_halo, 0, SIDES[0]),
        copy(wide.at[:, pl.ds(2, 2)], wide.at[:, pl.ds(10, 2)], send_halo, recv_halo, 1, SIDES[1]),
        copy(edge_send.at[0], edge_recv.at[0], send_halo, recv_halo, 2, SIDES[2]),
        copy(edge_send.at[1], edge_recv.at[1], send_halo, recv_halo, 3, SIDES[3]),
    ]
    start(halo, SIDES)

    high, low = split(wide[0:4, 2:10].reshape(4 * rows, depth))
    grid_pieces[...] = jnp.concatenate([high, low], axis=0).astype(BF16)
    for one in loads[4:]:
        one.wait()

    def exchange(turn):
        here = slice(turn * CHUNK, turn * CHUNK + CHUNK)
        cells = cell[:, here]
        goal = target[:, here]
        diameter = size[:, here]
        moving = motion[:, 0, here]
        at_z = jnp.bitwise_and(cells, depth - 1)
        at_xy = lax.shift_right_logical(cells, 8)
        hot_z = (lax.broadcasted_iota(jnp.int32, (depth, CHUNK), 0) == at_z).astype(F32).astype(BF16)
        hot_xy = (lax.broadcasted_iota(jnp.int32, (rows, CHUNK), 0) == at_xy).astype(F32)
        found = jnp.dot(grid_pieces[...], hot_z, preferred_element_type=F32)
        found = found[: 4 * rows] + found[4 * rows :]
        local = jnp.concatenate(
            [jnp.sum(found[f * rows : (f + 1) * rows] * hot_xy, axis=0, keepdims=True) for f in range(4)], axis=0
        )
        gap = local - moving
        field = lax.broadcasted_iota(jnp.int32, gap.shape, 0)
        pace = jnp.where(field == 3, TIME_STEP / HEAT_TIME, TIME_STEP / DRAG_TIME)
        fall = jnp.where(field == 2, TIME_STEP * GRAVITY, 0.0)
        carried = moving + pace * gap - fall
        vapour = VAPOUR_RATE * diameter * (1.0 / (1.0 + jnp.exp(-gap[3:4])))
        fresh = jnp.concatenate([carried, diameter - TIME_STEP * vapour], axis=0)
        renewed[0:5, here] = fresh
        kept[:, 0, here] = jnp.where(goal == 4, fresh, 0.0)
        alive = goal >= 0
        drag = jnp.where(alive, -DRAG_COUPLING * diameter * diameter * gap[2:3], 0.0)
        vapour = jnp.where(alive, vapour, 0.0)
        drag_high, drag_low = split(drag)
        vapour_high, vapour_low = split(vapour)
        spread = jnp.concatenate(
            [hot_xy * drag_high, hot_xy * vapour_high, hot_xy * drag_low, hot_xy * vapour_low], axis=0
        ).astype(BF16)
        summed[...] += lax.dot_general(spread, hot_z, NT, preferred_element_type=F32)

    turns = slots // CHUNK
    exchange(0)

    tile_row = lax.broadcasted_iota(jnp.int32, (8, 256), 0)

    def layer(dx, i):
        return 8 - i if dx > 0 else i - 1

    def blocks(buffer, which, send, recv):
        block = buffer[own]
        for way, (dx, dy) in enumerate(CORNERS):
            for i in range(1, 5):
                near, far = block[layer(dx, i)], block[layer(dx, 9 - i)]
                if i > 1:
                    if dy > 0:
                        near = jnp.where(tile_row >= i, near, pltpu.roll(far, i - 1, 0))
                    else:
                        near = jnp.where(tile_row < 8 - i, near, pltpu.roll(far, 9 - i, 0))
                corner_send[which, way, i - 1] = near
        copies = [
            copy(
                buffer.at[own], buffer.at[pl.ds(8 - 8 * dx, 8), there(dy)],
                send, recv, spot, (dx, dy),
            )
            for spot, (dx, dy) in enumerate(SIDES)
        ]
        copies += [
            copy(corner_send.at[which, way], corner_recv.at[which, way], send, recv, 4 + way, side)
            for way, side in enumerate(CORNERS)
        ]
        start(copies, AROUND)
        return copies

    def unpack(buffer, which):
        for way, (dx, dy) in enumerate(CORNERS):
            def place():
                base, side = 8 - 8 * dx, here_from(dy)
                for i in range(1, 5):
                    tile = corner_recv[which, way, i - 1]
                    buffer[base + layer(dx, i), side] = tile
                    back = (9 - i if dy > 0 else i - 1) % 8
                    buffer[base + layer(dx, 9 - i), side] = pltpu.roll(tile, back, 0) if back else tile

            if pair:
                pl.when(exists(0, -dy))(place)
            else:
                place()

    receive(border, SIDES)
    guess[:, 7:8] = side_recv[0]
    guess[:, 16:17] = side_recv[1]
    sums[own] = (
        rim[2:10] + rim[0:8] + guess[:, 9:17] + guess[:, 7:15]
        + along_depth(rim[1:9], 1) + along_depth(rim[1:9], -1)
    )
    sum_copies = blocks(sums, 0, send_sum, recv_sum)

    for turn in range(1, turns - 1):
        exchange(turn)

    receive(halo, SIDES)
    for f in range(5):
        tall[f, :, 6:8] = edge_recv[0, f]
        tall[f, :, 16:18] = edge_recv[1, f]
    def predict(f):
        centre = wide[f, 2:10]
        near_x, near_x2 = wide[f, 3:11], wide[f, 1:9]
        near_y, near_y2 = tall[f, :, 9:17], tall[f, :, 7:15]
        near_z, near_z2 = along_depth(centre, -1), along_depth(centre, 1)
        laplace = near_x + near_x2 + near_y + near_y2 + near_z + near_z2 - 6.0 * centre
        slope_x = 8.0 * (near_x - near_x2) - (wide[f, 4:12] - wide[f, 0:8])
        slope_y = 8.0 * (near_y - near_y2) - (tall[f, :, 10:18] - tall[f, :, 6:14])
        slope_z = 8.0 * (near_z - near_z2) - (along_depth(centre, -2) - along_depth(centre, 2))
        transport = (wide[0, 2:10] * slope_x + wide[1, 2:10] * slope_y + wide[2, 2:10] * slope_z) * (1.0 / 12.0)
        star[f] = centre + TIME_STEP * (DIFFUSION * laplace - transport)

    for f in range(3):
        predict(f)
        if f == 1:
            tall_v[:, 8:16] = star[1]
            v_send[0] = star[1, :, 7:8]
            v_send[1] = star[1, :, 0:1]
            u_halo[2] = star[0, 7]
            u_halo[3] = star[0, 0]
            edges = [
                copy(u_halo.at[2], u_halo.at[0], send_star, recv_star, 0, SIDES[0]),
                copy(u_halo.at[3], u_halo.at[1], send_star, recv_star, 1, SIDES[1]),
                copy(v_send.at[0], v_recv.at[0], send_star, recv_star, 2, SIDES[2]),
                copy(v_send.at[1], v_recv.at[1], send_star, recv_star, 3, SIDES[3]),
            ]
            start(edges, SIDES)

    numbers = lax.broadcasted_iota(jnp.int32, (rows, depth), 0) * depth + lax.broadcasted_iota(
        jnp.int32, (rows, depth), 1
    )
    ramp = jnp.clip((CLOCK - spray_time[...].astype(F32)) / SPRAY_RAMP, 0.0, 1.0)
    strength = SPRAY_RATE * ramp * spray_on[...].astype(F32)
    spray = jnp.zeros((rows, depth), F32)
    for head in range(spray_on.shape[1]):
        spray += jnp.where(numbers == spray_cell[:, head : head + 1], strength[:, head : head + 1], 0.0)
    exchange(turns - 1)

    total = summed[...]
    drag = total[:rows] + total[2 * rows : 3 * rows]
    vapour = total[rows : 2 * rows] + total[3 * rows :]
    lift = star[2] + (TIME_STEP * (drag - spray)).reshape(8, 8, 256)
    star[2] = lift

    receive(edges, SIDES)
    tall_v[:, 7:8] = v_recv[0]
    tall_v[:, 16:17] = v_recv[1]
    speed = star[0]
    spread_x = jnp.concatenate([speed[1:8], u_halo[1:2]], axis=0) - jnp.concatenate(
        [u_halo[0:1], speed[0:7]], axis=0
    )
    spread = spread_x + (tall_v[:, 9:17] - tall_v[:, 7:15]) + (along_depth(lift, -1) - along_depth(lift, 1))
    parts[own] = spread * (0.5 / TIME_STEP)
    part_copies = blocks(parts, 1, send_src, recv_src)

    predict(3)
    predict(4)
    star[3] = star[3] + (TIME_STEP * (-LATENT * vapour - spray)).reshape(8, 8, 256)
    star[4] = star[4] + (TIME_STEP * vapour).reshape(8, 8, 256)

    early = [
        pltpu.make_async_copy(star.at[pl.ds(3, 2)], gas_next.at[pl.ds(3, 2)], send_out.at[0]),
        pltpu.make_async_copy(kept, kept_hbm, send_out.at[1]),
    ]
    for one in early:
        one.start()

    upper = (
        lax.broadcasted_iota(jnp.int32, (256, 256), 0) <= lax.broadcasted_iota(jnp.int32, (256, 256), 1)
    ).astype(F32).astype(BF16)
    eight = lax.broadcasted_iota(jnp.int32, (8, 256), 0)

    def pack(turn, carry):
        here = pl.ds(pl.multiple_of(turn * CHUNK, CHUNK), CHUNK)
        goal = target[:, here]
        pieces = [(eight == goal[:, k * 256 : k * 256 + 256]).astype(F32) for k in range(CHUNK // 256)]
        counts = jnp.dot(jnp.concatenate(pieces, axis=0).astype(BF16), upper, preferred_element_type=F32)
        places = []
        for k, piece in enumerate(pieces):
            count = counts[8 * k : 8 * k + 8] + carry
            carry = count[:, 255:256]
            place = jnp.where(eight < 4, piece * (count + (512.0 * eight.astype(F32))), 0.0)
            places.append(jnp.sum(place, axis=0, keepdims=True))
        place = jnp.concatenate(places, axis=1).astype(jnp.int32) - 1
        hot_low = (
            lax.broadcasted_iota(jnp.int32, (256, CHUNK), 0) == jnp.bitwise_and(place, 255)
        ).astype(F32).astype(BF16)
        hot_high = (
            lax.broadcasted_iota(jnp.int32, (8, CHUNK), 0) == lax.shift_right_arithmetic(place, 8)
        ).astype(F32)
        top, rest = split(renewed[0:5, here])
        bundle = jnp.concatenate(
            [hot_high * top[f : f + 1] for f in range(5)] + [hot_high * rest[f : f + 1] for f in range(5)], axis=0
        ).astype(BF16)
        packed[...] += lax.dot_general(bundle, hot_low, NT, preferred_element_type=F32)
        return carry

    lax.fori_loop(0, turns, pack, jnp.zeros((8, 1), F32))
    bundle = packed[0:40] + packed[40:80]
    for f in range(5):
        for way in range(4):
            for half in range(2):
                spot = f * 8 + 2 * way + half
                parcels[way, f : f + 1, half * 256 : half * 256 + 256] = bundle[spot : spot + 1]
    for way in range(4):
        parcels[way, 5:8] = jnp.zeros((3, 512), F32)
    parcel = [
        copy(parcels.at[way], landed.at[way], send_parcel, recv_parcel, way, SIDES[way]) for way in range(4)
    ]
    start(parcel, SIDES)

    receive(sum_copies, AROUND)
    unpack(sums, 0)
    receive(part_copies, AROUND)
    unpack(parts, 1)

    for x in range(0, 24, 4):
        swap[0, x : x + 4] = (sums[x : x + 4] - parts[x : x + 4]) * factors[x // 8]
    for turn in range(1, ITERS):
        old, new = swap.at[(turn - 1) % 2], swap.at[turn % 2]
        x = turn
        while x < 24 - turn:
            end = min(x + (4 if pair else 2), 24 - turn, (x // 8 + 1) * 8)
            centre = old[x:end]
            total = old[x - 1 : end - 1] + old[x + 1 : end + 1]
            total = total + along_rows(centre, 1) + along_rows(centre, -1)
            total = total + along_depth(centre, 1) + along_depth(centre, -1)
            new[x:end] = (total - parts[x:end]) * factors[x // 8]
            x = end

    last = swap.at[(ITERS - 1) % 2]
    centre = last[own]
    final[...] = centre
    half = TIME_STEP * 0.5
    star[0] = star[0] - half * (last[9:17, pl.ds(own_y, 8)] - last[7:15, pl.ds(own_y, 8)])
    star[2] = star[2] - half * (along_depth(centre, -1) - along_depth(centre, 1))
    middle = last[8:16]
    spare = swap.at[ITERS % 2]
    spare[8:16] = along_rows(middle, -1) - along_rows(middle, 1)
    star[1] = star[1] - half * spare[own]
    late = [
        pltpu.make_async_copy(star.at[pl.ds(0, 3)], gas_next.at[pl.ds(0, 3)], send_out.at[2]),
        pltpu.make_async_copy(final, pressure, send_out.at[3]),
    ]
    for one in late:
        one.start()
    receive(parcel, SIDES)
    for way in range(4):
        arrived[way, :, 0, :] = landed[way, 0:5]
    late.append(pltpu.make_async_copy(arrived, arrived_hbm, send_out.at[4]))
    late[2].start()

    sent(border, SIDES)
    sent(halo, SIDES)
    sent(edges, SIDES)
    sent(sum_copies, AROUND)
    sent(part_copies, AROUND)
    sent(parcel, SIDES)
    for one in early + late:
        one.wait()


def hand_over_kernel(*refs):
    sems = refs[-1]
    into = [pltpu.make_async_copy(refs[k], refs[8 + k], sems.at[k]) for k in range(4)]
    out = [pltpu.make_async_copy(refs[8 + k], refs[4 + k], sems.at[4 + k]) for k in range(4)]
    for one in into:
        one.start()
    for k in (3, 1, 2, 0):
        into[k].wait()
        out[k].start()
    for one in out:
        one.wait()


def body(
    n_gx, n_gy,
    gas_state, pressure_guess, drop_motion, drop_size, drop_cell, drop_target, spray_on, spray_time, spray_cell,
):
    hbm = pl.BlockSpec(memory_space=pltpu.HBM)
    dma = pltpu.SemaphoreType.DMA
    slots = drop_size.shape[1]
    heads = spray_on.shape[1]
    tall_rows = 16 if n_gy == 2 else 24
    block = gas_state.shape[1:]
    shape = functools.partial(jax.ShapeDtypeStruct, dtype=F32)
    outs = (shape(gas_state.shape), shape(block), shape((5, 1, slots)), shape((4, 5, 1, 512)))
    results = pl.pallas_call(
        functools.partial(evolve_kernel, n_gx, n_gy),
        out_shape=outs,
        in_specs=[hbm] * 9,
        out_specs=(hbm,) * 4,
        scratch_shapes=[
            pltpu.VMEM(gas_state.shape, F32),
            pltpu.VMEM((5, 1, slots), F32),
            pltpu.VMEM((4, 5, 1, 512), F32),
            pltpu.VMEM((2, 24, tall_rows, 256), F32),
            pltpu.VMEM(block, F32),
            pltpu.VMEM(drop_motion.shape, F32),
            pltpu.VMEM((1, slots), F32),
            pltpu.VMEM((1, slots), jnp.int32),
            pltpu.VMEM((1, slots), jnp.int32),
            pltpu.VMEM((1, heads), jnp.int32),
            pltpu.VMEM((1, heads), jnp.int32),
            pltpu.VMEM((1, heads), jnp.int32),
            pltpu.VMEM((512, 256), BF16),
            pltpu.VMEM((256, 256), F32),
            pltpu.VMEM((80, 256), F32),
            pltpu.VMEM((8, slots), F32),
            pltpu.VMEM((4, 8, 512), F32),
            pltpu.VMEM((4, 8, 512), F32),
            pltpu.VMEM((8, 24, 256), F32),
            pltpu.VMEM((10, 8, 256), F32),
            pltpu.VMEM((2, 8, 1, 256), F32),
            pltpu.VMEM((2, 8, 1, 256), F32),
            pltpu.VMEM((5, 12, 8, 256), F32),
            pltpu.VMEM((5, 8, 24, 256), F32),
            pltpu.VMEM((2, 5, 8, 2, 256), F32),
            pltpu.VMEM((2, 5, 8, 2, 256), F32),
            pltpu.VMEM((24, tall_rows, 256), F32),
            pltpu.VMEM((24, tall_rows, 256), F32),
            pltpu.VMEM((2, 4, 4, 8, 256), F32),
            pltpu.VMEM((2, 4, 4, 8, 256), F32),
            pltpu.VMEM((8, 24, 256), F32),
            pltpu.VMEM((4, 8, 256), F32),
            pltpu.VMEM((2, 8, 1, 256), F32),
            pltpu.VMEM((2, 8, 1, 256), F32),
        ]
        + [dma((11,)), dma((5,))] + [dma((4,))] * 8 + [dma((8,))] * 4,
        compiler_params=pltpu.CompilerParams(
            collective_id=0, has_side_effects=True, vmem_limit_bytes=60 * 1024 * 1024
        ),
    )(
        gas_state, pressure_guess, drop_motion, drop_size, drop_cell, drop_target, spray_on, spray_time, spray_cell
    )
    return pl.pallas_call(
        hand_over_kernel,
        out_shape=outs,
        in_specs=[hbm] * 4,
        out_specs=(hbm,) * 4,
        scratch_shapes=[pltpu.VMEM(one.shape, F32) for one in outs] + [dma((8,))],
        compiler_params=pltpu.CompilerParams(vmem_limit_bytes=60 * 1024 * 1024),
    )(*results)


def solution(mesh):
    in_specs = (
        P(None, "gx", "gy", None),
        P("gx", "gy", None),
        P(None, "gx", "gy"),
    ) + (P("gx", "gy"),) * 6
    out_specs = (
        P(None, "gx", "gy", None),
        P("gx", "gy", None),
        P(None, "gx", "gy"),
        P(None, None, "gx", "gy"),
    )
    inner = functools.partial(body, mesh.shape["gx"], mesh.shape["gy"])
    return jax.shard_map(inner, mesh=mesh, in_specs=in_specs, out_specs=out_specs, check_vma=False)
```

```python
import functools

import jax
import jax.numpy as jnp
from jax import lax
from jax.experimental import pallas as pl
from jax.experimental.pallas import tpu as pltpu
from jax.sharding import PartitionSpec as P

ITERS = 8
TIME_STEP = 0.2
DIFFUSION = 0.1
DRAG_TIME = 0.5
HEAT_TIME = 1.0
GRAVITY = 1.0
VAPOUR_RATE = 0.5
DRAG_COUPLING = 0.5
LATENT = 2.0
SPRAY_RATE = 3.0
CLOCK = 100.0
SPRAY_RAMP = 50.0

MESH = pl.DeviceIdType.MESH
F32 = jnp.float32
BF16 = jnp.bfloat16
CHUNK = 1024
NT = (((1,), (1,)), ((), ()))
SIDES = ((1, 0), (-1, 0), (0, 1), (0, -1))
CORNERS = ((1, 1), (1, -1), (-1, 1), (-1, -1))
AROUND = SIDES + CORNERS


def split(values):
    high = values.astype(BF16).astype(F32)
    return high, values - high


def along_depth(values, by):
    lane = lax.broadcasted_iota(jnp.int32, (1, 1, 128), 2)
    first = pltpu.roll(values[:, :, :128], by % 128, 2)
    second = pltpu.roll(values[:, :, 128:], by % 128, 2)
    if by > 0:
        return jnp.concatenate(
            [jnp.where(lane < by, 0.0, first), jnp.where(lane < by, first, second)], axis=2
        )
    inside = lane < 128 + by
    return jnp.concatenate([jnp.where(inside, first, second), jnp.where(inside, second, 0.0)], axis=2)


def along_rows(values, by):
    row = lax.broadcasted_iota(jnp.int32, (1, 8, 256), 1)
    edge = row == (0 if by > 0 else 7)
    tiles = [pltpu.roll(values[:, k : k + 8], by % 8, 1) for k in range(0, values.shape[1], 8)]
    beside = [0.0] + tiles[:-1] if by > 0 else tiles[1:] + [0.0]
    return jnp.concatenate([jnp.where(edge, other, tile) for tile, other in zip(tiles, beside)], axis=1)


def evolve_kernel(
    n_gx, n_gy,
    gas_hbm, guess_hbm, motion_hbm, size_hbm, cell_hbm, target_hbm, on_hbm, time_hbm, place_hbm,
    gas_next, pressure, kept_hbm, arrived_hbm,
    star, kept, arrived, swap, final,
    motion, size, cell, target, spray_on, spray_time, spray_cell,
    grid_pieces, summed, packed, renewed, parcels, landed,
    guess, rim, side_send, side_recv, wide, tall, edge_send, edge_recv, sums, parts, corner_send, corner_recv, tall_v, u_halo, v_send, v_recv,
    send_in, send_out, send_rim, recv_rim, send_halo, recv_halo, send_star, recv_star, send_parcel, recv_parcel, send_sum, recv_sum, send_src,
    recv_src,
):
    me_x, me_y = lax.axis_index("gx"), lax.axis_index("gy")
    slots = size.shape[1]
    rows, depth = 64, 256
    pair = n_gy == 2
    tall_rows = sums.shape[1]
    own_y = pl.multiple_of(me_y * 8, 8) if pair else 8
    own = (pl.ds(8, 8), pl.ds(own_y, 8))

    def there(dy):
        return pl.ds(own_y, 8) if pair else pl.ds(8 - 8 * dy, 8)

    def here_from(dy):
        if pair:
            return pl.ds(own_y if dy == 0 else pl.multiple_of((1 - me_y) * 8, 8), 8)
        return pl.ds(8 - 8 * dy, 8)

    def exists(dx, dy):
        to_x, to_y = me_x + dx, me_y + dy
        return (to_x >= 0) & (to_x < n_gx) & (to_y >= 0) & (to_y < n_gy)

    def device(dx, dy):
        return {"gx": jnp.clip(me_x + dx, 0, n_gx - 1), "gy": jnp.clip(me_y + dy, 0, n_gy - 1)}

    def copy(src, dst, send, recv, spot, side):
        return pltpu.make_async_remote_copy(
            src_ref=src, dst_ref=dst, send_sem=send.at[spot], recv_sem=recv.at[spot],
            device_id=device(*side), device_id_type=MESH,
        )

    def start(copies, sides):
        for one, (dx, dy) in zip(copies, sides):
            pl.when(exists(dx, dy))(one.start)

    def receive(copies, sides):
        for one, (dx, dy) in zip(copies, sides):
            pl.when(exists(-dx, -dy))(one.wait_recv)

    def sent(copies, sides):
        for one, (dx, dy) in zip(copies, sides):
            pl.when(exists(dx, dy))(one.wait_send)

    loads = [
        pltpu.make_async_copy(src, dst, send_in.at[spot])
        for spot, (src, dst) in enumerate(
            (
                (guess_hbm, rim.at[pl.ds(1, 8)]),
                (guess_hbm, guess.at[:, pl.ds(8, 8)]),
                (gas_hbm, wide.at[:, pl.ds(2, 8)]),
                (gas_hbm, tall.at[:, :, pl.ds(8, 8)]),
                (cell_hbm, cell),
                (motion_hbm, motion),
                (size_hbm, size),
                (target_hbm, target),
                (on_hbm, spray_on),
                (time_hbm, spray_time),
                (place_hbm, spray_cell),
            )
        )
    ]
    for one in loads:
        one.start()

    barrier = pltpu.get_barrier_semaphore()
    for dx, dy in AROUND:
        @pl.when(exists(dx, dy))
        def _():
            pl.semaphore_signal(barrier, inc=1, device_id=device(dx, dy), device_id_type=MESH)

    @pl.when(~exists(-1, 0))
    def _():
        wide[:, 0:2] = jnp.zeros((5, 2, 8, 256), F32)
        rim[0] = jnp.zeros((8, 256), F32)
        u_halo[0] = jnp.zeros((8, 256), F32)

    @pl.when(~exists(1, 0))
    def _():
        wide[:, 10:12] = jnp.zeros((5, 2, 8, 256), F32)
        rim[9] = jnp.zeros((8, 256), F32)
        u_halo[1] = jnp.zeros((8, 256), F32)

    @pl.when(~exists(0, -1))
    def _():
        edge_recv[0] = jnp.zeros((5, 8, 2, 256), F32)
        side_recv[0] = jnp.zeros((8, 1, 256), F32)
        v_recv[0] = jnp.zeros((8, 1, 256), F32)

    @pl.when(~exists(0, 1))
    def _():
        edge_recv[1] = jnp.zeros((5, 8, 2, 256), F32)
        side_recv[1] = jnp.zeros((8, 1, 256), F32)
        v_recv[1] = jnp.zeros((8, 1, 256), F32)

    for way, (dx, dy) in enumerate(SIDES):
        @pl.when(~exists(-dx, -dy))
        def _():
            landed[way] = jnp.zeros((8, 512), F32)
            if dy == 0 or not pair:
                spot = (pl.ds(8 - 8 * dx, 8), here_from(dy))
                sums[spot] = jnp.zeros((8, 8, 256), F32)
                parts[spot] = jnp.zeros((8, 8, 256), F32)

    for way, (dx, dy) in enumerate(CORNERS):
        @pl.when(~exists(-dx, -dy))
        def _():
            corner_recv[0, way] = jnp.zeros((4, 8, 256), F32)
            corner_recv[1, way] = jnp.zeros((4, 8, 256), F32)

    low_x, high_x = exists(-1, 0).astype(F32), exists(1, 0).astype(F32)
    if pair:
        factors = [low_x * (1.0 / 6.0), 1.0 / 6.0, high_x * (1.0 / 6.0)]
    else:
        row = lax.broadcasted_iota(jnp.int32, (1, tall_rows, 256), 1)
        low_y, high_y = exists(0, -1).astype(F32), exists(0, 1).astype(F32)
        factor = jnp.where(row < 8, low_y, jnp.where(row < 16, 1.0, high_y)) * (1.0 / 6.0)
        factors = [factor * low_x, factor, factor * high_x]
    summed[...] = jnp.zeros_like(summed)
    packed[...] = jnp.zeros_like(packed)

    for one in loads[0:4]:
        one.wait()
    side_send[0] = rim[1:9, 7:8]
    side_send[1] = rim[1:9, 0:1]
    for f in range(5):
        inner = wide[f, 2:10]
        edge_send[0, f] = inner[:, 6:8]
        edge_send[1, f] = inner[:, 0:2]
    pl.semaphore_wait(barrier, sum(exists(dx, dy).astype(jnp.int32) for dx, dy in AROUND))
    border = [
        copy(rim.at[8], rim.at[0], send_rim, recv_rim, 0, SIDES[0]),
        copy(rim.at[1], rim.at[9], send_rim, recv_rim, 1, SIDES[1]),
        copy(side_send.at[0], side_recv.at[0], send_rim, recv_rim, 2, SIDES[2]),
        copy(side_send.at[1], side_recv.at[1], send_rim, recv_rim, 3, SIDES[3]),
    ]
    start(border, SIDES)
    halo = [
        copy(wide.at[:, pl.ds(8, 2)], wide.at[:, pl.ds(0, 2)], send_halo, recv_halo, 0, SIDES[0]),
        copy(wide.at[:, pl.ds(2, 2)], wide.at[:, pl.ds(10, 2)], send_halo, recv_halo, 1, SIDES[1]),
        copy(edge_send.at[0], edge_recv.at[0], send_halo, recv_halo, 2, SIDES[2]),
        copy(edge_send.at[1], edge_recv.at[1], send_halo, recv_halo, 3, SIDES[3]),
    ]
    start(halo, SIDES)

    high, low = split(wide[0:4, 2:10].reshape(4 * rows, depth))
    grid_pieces[...] = jnp.concatenate([high, low], axis=0).astype(BF16)
    for one in loads[4:]:
        one.wait()

    def exchange(turn):
        here = slice(turn * CHUNK, turn * CHUNK + CHUNK)
        cells = cell[:, here]
        goal = target[:, here]
        diameter = size[:, here]
        moving = motion[:, 0, here]
        at_z = jnp.bitwise_and(cells, depth - 1)
        at_xy = lax.shift_right_logical(cells, 8)
        hot_z = (lax.broadcasted_iota(jnp.int32, (depth, CHUNK), 0) == at_z).astype(F32).astype(BF16)
        hot_xy = (lax.broadcasted_iota(jnp.int32, (rows, CHUNK), 0) == at_xy).astype(F32)
        found = jnp.dot(grid_pieces[0:256], hot_z, preferred_element_type=F32) + jnp.dot(
            grid_pieces[256:512], hot_z, preferred_element_type=F32
        )
        local = jnp.concatenate(
            [jnp.sum(found[f * rows : (f + 1) * rows] * hot_xy, axis=0, keepdims=True) for f in range(4)], axis=0
        )
        gap = local - moving
        field = lax.broadcasted_iota(jnp.int32, gap.shape, 0)
        pace = jnp.where(field == 3, TIME_STEP / HEAT_TIME, TIME_STEP / DRAG_TIME)
        fall = jnp.where(field == 2, TIME_STEP * GRAVITY, 0.0)
        carried = moving + pace * gap - fall
        vapour = VAPOUR_RATE * diameter * (1.0 / (1.0 + jnp.exp(-gap[3:4])))
        fresh = jnp.concatenate([carried, diameter - TIME_STEP * vapour], axis=0)
        renewed[0:5, here] = fresh
        kept[:, 0, here] = jnp.where(goal == 4, fresh, 0.0)
        alive = goal >= 0
        drag = jnp.where(alive, -DRAG_COUPLING * diameter * diameter * gap[2:3], 0.0)
        vapour = jnp.where(alive, vapour, 0.0)
        drag_high, drag_low = split(drag)
        vapour_high, vapour_low = split(vapour)
        spread = jnp.concatenate(
            [hot_xy * drag_high, hot_xy * vapour_high, hot_xy * drag_low, hot_xy * vapour_low], axis=0
        ).astype(BF16)
        summed[...] += lax.dot_general(spread, hot_z, NT, preferred_element_type=F32)

    turns = slots // CHUNK
    exchange(0)

    tile_row = lax.broadcasted_iota(jnp.int32, (8, 256), 0)

    def layer(dx, i):
        return 8 - i if dx > 0 else i - 1

    def blocks(buffer, which, send, recv):
        copies = [
            copy(buffer.at[own], buffer.at[pl.ds(8 - 8 * dx, 8), there(dy)], send, recv, spot, (dx, dy))
            for spot, (dx, dy) in enumerate(SIDES)
        ]
        start(copies[2:] + copies[:2], SIDES[2:] + SIDES[:2])
        block = buffer[own]
        for way, (dx, dy) in enumerate(CORNERS):
            for i in range(1, 5):
                near, far = block[layer(dx, i)], block[layer(dx, 9 - i)]
                if i > 1:
                    if dy > 0:
                        near = jnp.where(tile_row >= i, near, pltpu.roll(far, i - 1, 0))
                    else:
                        near = jnp.where(tile_row < 8 - i, near, pltpu.roll(far, 9 - i, 0))
                corner_send[which, way, i - 1] = near
        corners = [
            copy(corner_send.at[which, way], corner_recv.at[which, way], send, recv, 4 + way, side)
            for way, side in enumerate(CORNERS)
        ]
        start(corners, CORNERS)
        return copies + corners

    def unpack(buffer, which):
        for way, (dx, dy) in enumerate(CORNERS):
            def place():
                base, side = 8 - 8 * dx, here_from(dy)
                for i in range(1, 5):
                    tile = corner_recv[which, way, i - 1]
                    buffer[base + layer(dx, i), side] = tile
                    back = (9 - i if dy > 0 else i - 1) % 8
                    buffer[base + layer(dx, 9 - i), side] = pltpu.roll(tile, back, 0) if back else tile

            if pair:
                pl.when(exists(0, -dy))(place)
            else:
                place()

    receive(border, SIDES)
    guess[:, 7:8] = side_recv[0]
    guess[:, 16:17] = side_recv[1]
    sums[own] = (
        rim[2:10] + rim[0:8] + guess[:, 9:17] + guess[:, 7:15]
        + along_depth(rim[1:9], 1) + along_depth(rim[1:9], -1)
    )
    sum_copies = blocks(sums, 0, send_sum, recv_sum)

    for turn in range(1, turns - 1):
        exchange(turn)

    receive(halo, SIDES)
    for f in range(5):
        tall[f, :, 6:8] = edge_recv[0, f]
        tall[f, :, 16:18] = edge_recv[1, f]
    def predict(f):
        centre = wide[f, 2:10]
        near_x, near_x2 = wide[f, 3:11], wide[f, 1:9]
        near_y, near_y2 = tall[f, :, 9:17], tall[f, :, 7:15]
        near_z, near_z2 = along_depth(centre, -1), along_depth(centre, 1)
        laplace = near_x + near_x2 + near_y + near_y2 + near_z + near_z2 - 6.0 * centre
        slope_x = 8.0 * (near_x - near_x2) - (wide[f, 4:12] - wide[f, 0:8])
        slope_y = 8.0 * (near_y - near_y2) - (tall[f, :, 10:18] - tall[f, :, 6:14])
        slope_z = 8.0 * (near_z - near_z2) - (along_depth(centre, -2) - along_depth(centre, 2))
        transport = (wide[0, 2:10] * slope_x + wide[1, 2:10] * slope_y + wide[2, 2:10] * slope_z) * (1.0 / 12.0)
        star[f] = centre + TIME_STEP * (DIFFUSION * laplace - transport)

    for f in range(3):
        predict(f)
        if f == 1:
            tall_v[:, 8:16] = star[1]
            v_send[0] = star[1, :, 7:8]
            v_send[1] = star[1, :, 0:1]
            u_halo[2] = star[0, 7]
            u_halo[3] = star[0, 0]
            edges = [
                copy(u_halo.at[2], u_halo.at[0], send_star, recv_star, 0, SIDES[0]),
                copy(u_halo.at[3], u_halo.at[1], send_star, recv_star, 1, SIDES[1]),
                copy(v_send.at[0], v_recv.at[0], send_star, recv_star, 2, SIDES[2]),
                copy(v_send.at[1], v_recv.at[1], send_star, recv_star, 3, SIDES[3]),
            ]
            start(edges, SIDES)

    numbers = lax.broadcasted_iota(jnp.int32, (rows, depth), 0) * depth + lax.broadcasted_iota(
        jnp.int32, (rows, depth), 1
    )
    ramp = jnp.clip((CLOCK - spray_time[...].astype(F32)) / SPRAY_RAMP, 0.0, 1.0)
    strength = SPRAY_RATE * ramp * spray_on[...].astype(F32)
    spray = jnp.zeros((rows, depth), F32)
    for head in range(spray_on.shape[1]):
        spray += jnp.where(numbers == spray_cell[:, head : head + 1], strength[:, head : head + 1], 0.0)
    exchange(turns - 1)

    total = summed[...]
    drag = total[:rows] + total[2 * rows : 3 * rows]
    vapour = total[rows : 2 * rows] + total[3 * rows :]
    lift = star[2] + (TIME_STEP * (drag - spray)).reshape(8, 8, 256)
    star[2] = lift

    receive(edges, SIDES)
    tall_v[:, 7:8] = v_recv[0]
    tall_v[:, 16:17] = v_recv[1]
    speed = star[0]
    spread_x = jnp.concatenate([speed[1:8], u_halo[1:2]], axis=0) - jnp.concatenate(
        [u_halo[0:1], speed[0:7]], axis=0
    )
    spread = spread_x + (tall_v[:, 9:17] - tall_v[:, 7:15]) + (along_depth(lift, -1) - along_depth(lift, 1))
    parts[own] = spread * (0.5 / TIME_STEP)
    part_copies = blocks(parts, 1, send_src, recv_src)

    predict(3)
    predict(4)
    star[3] = star[3] + (TIME_STEP * (-LATENT * vapour - spray)).reshape(8, 8, 256)
    star[4] = star[4] + (TIME_STEP * vapour).reshape(8, 8, 256)

    early = [
        pltpu.make_async_copy(star.at[pl.ds(3, 2)], gas_next.at[pl.ds(3, 2)], send_out.at[0]),
        pltpu.make_async_copy(kept, kept_hbm, send_out.at[1]),
    ]
    for one in early:
        one.start()

    upper = (
        lax.broadcasted_iota(jnp.int32, (256, 256), 0) <= lax.broadcasted_iota(jnp.int32, (256, 256), 1)
    ).astype(F32).astype(BF16)
    eight = lax.broadcasted_iota(jnp.int32, (8, 256), 0)

    def pack(turn, carry):
        here = slice(turn * CHUNK, turn * CHUNK + CHUNK)
        goal = target[:, here]
        pieces = [(eight == goal[:, k * 256 : k * 256 + 256]).astype(F32) for k in range(CHUNK // 256)]
        counts = jnp.dot(jnp.concatenate(pieces, axis=0).astype(BF16), upper, preferred_element_type=F32)
        places = []
        for k, piece in enumerate(pieces):
            count = counts[8 * k : 8 * k + 8] + carry
            carry = count[:, 255:256]
            place = jnp.where(eight < 4, piece * (count + (512.0 * eight.astype(F32))), 0.0)
            places.append(jnp.sum(place, axis=0, keepdims=True))
        place = jnp.concatenate(places, axis=1).astype(jnp.int32) - 1
        hot_low = (
            lax.broadcasted_iota(jnp.int32, (256, CHUNK), 0) == jnp.bitwise_and(place, 255)
        ).astype(F32).astype(BF16)
        hot_high = (
            lax.broadcasted_iota(jnp.int32, (8, CHUNK), 0) == lax.shift_right_arithmetic(place, 8)
        ).astype(F32)
        top, rest = split(renewed[0:5, here])
        bundle = jnp.concatenate(
            [hot_high * top[f : f + 1] for f in range(5)] + [hot_high * rest[f : f + 1] for f in range(5)], axis=0
        ).astype(BF16)
        packed[...] += lax.dot_general(bundle, hot_low, NT, preferred_element_type=F32)
        return carry

    carry = jnp.zeros((8, 1), F32)
    for turn in range(turns):
        carry = pack(turn, carry)
    bundle = packed[0:40] + packed[40:80]
    for f in range(5):
        for way in range(4):
            for half in range(2):
                spot = f * 8 + 2 * way + half
                parcels[way, f : f + 1, half * 256 : half * 256 + 256] = bundle[spot : spot + 1]
    for way in range(4):
        parcels[way, 5:8] = jnp.zeros((3, 512), F32)
    parcel = [
        copy(parcels.at[way], landed.at[way], send_parcel, recv_parcel, way, SIDES[way]) for way in range(4)
    ]
    start(parcel, SIDES)

    receive(sum_copies, AROUND)
    unpack(sums, 0)
    receive(part_copies, AROUND)
    unpack(parts, 1)

    for x in range(0, 24, 4):
        swap[0, x : x + 4] = (sums[x : x + 4] - parts[x : x + 4]) * factors[x // 8]
    for turn in range(1, ITERS):
        old, new = swap.at[(turn - 1) % 2], swap.at[turn % 2]
        x = turn
        while x < 24 - turn:
            end = min(x + (4 if pair else 2), 24 - turn, (x // 8 + 1) * 8)
            centre = old[x:end]
            total = old[x - 1 : end - 1] + old[x + 1 : end + 1]
            total = total + along_rows(centre, 1) + along_rows(centre, -1)
            total = total + along_depth(centre, 1) + along_depth(centre, -1)
            new[x:end] = (total - parts[x:end]) * factors[x // 8]
            x = end

    last = swap.at[(ITERS - 1) % 2]
    centre = last[own]
    final[...] = centre
    half = TIME_STEP * 0.5
    star[0] = star[0] - half * (last[9:17, pl.ds(own_y, 8)] - last[7:15, pl.ds(own_y, 8)])
    star[2] = star[2] - half * (along_depth(centre, -1) - along_depth(centre, 1))
    middle = last[8:16]
    spare = swap.at[ITERS % 2]
    spare[8:16] = along_rows(middle, -1) - along_rows(middle, 1)
    star[1] = star[1] - half * spare[own]
    late = [
        pltpu.make_async_copy(star.at[pl.ds(0, 3)], gas_next.at[pl.ds(0, 3)], send_out.at[2]),
        pltpu.make_async_copy(final, pressure, send_out.at[3]),
    ]
    for one in late:
        one.start()
    receive(parcel, SIDES)
    for way in range(4):
        arrived[way, :, 0, :] = landed[way, 0:5]
    late.append(pltpu.make_async_copy(arrived, arrived_hbm, send_out.at[4]))
    late[2].start()

    sent(border, SIDES)
    sent(halo, SIDES)
    sent(edges, SIDES)
    sent(sum_copies, AROUND)
    sent(part_copies, AROUND)
    sent(parcel, SIDES)
    for one in early + late:
        one.wait()


def hand_over_kernel(*refs):
    sems = refs[-1]
    into = [pltpu.make_async_copy(refs[k], refs[8 + k], sems.at[k]) for k in range(4)]
    out = [pltpu.make_async_copy(refs[8 + k], refs[4 + k], sems.at[4 + k]) for k in range(4)]
    for one in into:
        one.start()
    for k in (3, 1, 2, 0):
        into[k].wait()
        out[k].start()
    for one in out:
        one.wait()


def body(
    n_gx, n_gy,
    gas_state, pressure_guess, drop_motion, drop_size, drop_cell, drop_target, spray_on, spray_time, spray_cell,
):
    hbm = pl.BlockSpec(memory_space=pltpu.HBM)
    dma = pltpu.SemaphoreType.DMA
    slots = drop_size.shape[1]
    heads = spray_on.shape[1]
    tall_rows = 16 if n_gy == 2 else 24
    block = gas_state.shape[1:]
    shape = functools.partial(jax.ShapeDtypeStruct, dtype=F32)
    outs = (shape(gas_state.shape), shape(block), shape((5, 1, slots)), shape((4, 5, 1, 512)))
    results = pl.pallas_call(
        functools.partial(evolve_kernel, n_gx, n_gy),
        out_shape=outs,
        in_specs=[hbm] * 9,
        out_specs=(hbm,) * 4,
        scratch_shapes=[
            pltpu.VMEM(gas_state.shape, F32),
            pltpu.VMEM((5, 1, slots), F32),
            pltpu.VMEM((4, 5, 1, 512), F32),
            pltpu.VMEM((2, 24, tall_rows, 256), F32),
            pltpu.VMEM(block, F32),
            pltpu.VMEM(drop_motion.shape, F32),
            pltpu.VMEM((1, slots), F32),
            pltpu.VMEM((1, slots), jnp.int32),
            pltpu.VMEM((1, slots), jnp.int32),
            pltpu.VMEM((1, heads), jnp.int32),
            pltpu.VMEM((1, heads), jnp.int32),
            pltpu.VMEM((1, heads), jnp.int32),
            pltpu.VMEM((512, 256), BF16),
            pltpu.VMEM((256, 256), F32),
            pltpu.VMEM((80, 256), F32),
            pltpu.VMEM((8, slots), F32),
            pltpu.VMEM((4, 8, 512), F32),
            pltpu.VMEM((4, 8, 512), F32),
            pltpu.VMEM((8, 24, 256), F32),
            pltpu.VMEM((10, 8, 256), F32),
            pltpu.VMEM((2, 8, 1, 256), F32),
            pltpu.VMEM((2, 8, 1, 256), F32),
            pltpu.VMEM((5, 12, 8, 256), F32),
            pltpu.VMEM((5, 8, 24, 256), F32),
            pltpu.VMEM((2, 5, 8, 2, 256), F32),
            pltpu.VMEM((2, 5, 8, 2, 256), F32),
            pltpu.VMEM((24, tall_rows, 256), F32),
            pltpu.VMEM((24, tall_rows, 256), F32),
            pltpu.VMEM((2, 4, 4, 8, 256), F32),
            pltpu.VMEM((2, 4, 4, 8, 256), F32),
            pltpu.VMEM((8, 24, 256), F32),
            pltpu.VMEM((4, 8, 256), F32),
            pltpu.VMEM((2, 8, 1, 256), F32),
            pltpu.VMEM((2, 8, 1, 256), F32),
        ]
        + [dma((11,)), dma((5,))] + [dma((4,))] * 8 + [dma((8,))] * 4,
        compiler_params=pltpu.CompilerParams(
            collective_id=0, has_side_effects=True, vmem_limit_bytes=60 * 1024 * 1024
        ),
    )(
        gas_state, pressure_guess, drop_motion, drop_size, drop_cell, drop_target, spray_on, spray_time, spray_cell
    )
    return pl.pallas_call(
        hand_over_kernel,
        out_shape=outs,
        in_specs=[hbm] * 4,
        out_specs=(hbm,) * 4,
        scratch_shapes=[pltpu.VMEM(one.shape, F32) for one in outs] + [dma((8,))],
        compiler_params=pltpu.CompilerParams(vmem_limit_bytes=60 * 1024 * 1024),
    )(*results)


def solution(mesh):
    in_specs = (
        P(None, "gx", "gy", None),
        P("gx", "gy", None),
        P(None, "gx", "gy"),
    ) + (P("gx", "gy"),) * 6
    out_specs = (
        P(None, "gx", "gy", None),
        P("gx", "gy", None),
        P(None, "gx", "gy"),
        P(None, None, "gx", "gy"),
    )
    inner = functools.partial(body, mesh.shape["gx"], mesh.shape["gy"])
    return jax.shard_map(inner, mesh=mesh, in_specs=in_specs, out_specs=out_specs, check_vma=False)
```

```python
import functools

import jax
import jax.numpy as jnp
from jax import lax
from jax.experimental import pallas as pl
from jax.experimental.pallas import tpu as pltpu
from jax.sharding import PartitionSpec as P

ITERS = 8
TIME_STEP = 0.2
DIFFUSION = 0.1
DRAG_TIME = 0.5
HEAT_TIME = 1.0
GRAVITY = 1.0
VAPOUR_RATE = 0.5
DRAG_COUPLING = 0.5
LATENT = 2.0
SPRAY_RATE = 3.0
CLOCK = 100.0
SPRAY_RAMP = 50.0

MESH = pl.DeviceIdType.MESH
F32 = jnp.float32
BF16 = jnp.bfloat16
CHUNK = 1024
NT = (((1,), (1,)), ((), ()))
SIDES = ((1, 0), (-1, 0), (0, 1), (0, -1))
CORNERS = ((1, 1), (1, -1), (-1, 1), (-1, -1))
AROUND = SIDES + CORNERS


def split(values):
    high = values.astype(BF16).astype(F32)
    return high, values - high


def along_depth(values, by):
    lane = lax.broadcasted_iota(jnp.int32, (1, 1, 128), 2)
    first = pltpu.roll(values[:, :, :128], by % 128, 2)
    second = pltpu.roll(values[:, :, 128:], by % 128, 2)
    if by > 0:
        return jnp.concatenate(
            [jnp.where(lane < by, 0.0, first), jnp.where(lane < by, first, second)], axis=2
        )
    inside = lane < 128 + by
    return jnp.concatenate([jnp.where(inside, first, second), jnp.where(inside, second, 0.0)], axis=2)


def along_rows(values, by):
    row = lax.broadcasted_iota(jnp.int32, (1, 8, 256), 1)
    edge = row == (0 if by > 0 else 7)
    tiles = [pltpu.roll(values[:, k : k + 8], by % 8, 1) for k in range(0, values.shape[1], 8)]
    beside = [0.0] + tiles[:-1] if by > 0 else tiles[1:] + [0.0]
    return jnp.concatenate([jnp.where(edge, other, tile) for tile, other in zip(tiles, beside)], axis=1)


def evolve_kernel(
    n_gx, n_gy,
    gas_hbm, guess_hbm, motion_hbm, size_hbm, cell_hbm, target_hbm, on_hbm, time_hbm, place_hbm,
    gas_next, pressure, kept_hbm, arrived_hbm,
    star, kept, arrived, swap, final,
    motion, size, cell, target, spray_on, spray_time, spray_cell,
    grid_pieces, summed, packed, renewed, parcels, landed,
    guess, rim, side_send, side_recv, wide, tall, edge_send, edge_recv, sums, parts, corner_send, corner_recv, tall_v, u_halo, v_send, v_recv,
    send_in, send_out, send_rim, recv_rim, send_halo, recv_halo, send_star, recv_star, send_parcel, recv_parcel, send_sum, recv_sum, send_src,
    recv_src,
):
    me_x, me_y = lax.axis_index("gx"), lax.axis_index("gy")
    slots = size.shape[1]
    rows, depth = 64, 256
    pair = n_gy == 2
    tall_rows = sums.shape[1]
    own_y = pl.multiple_of(me_y * 8, 8) if pair else 8
    own = (pl.ds(8, 8), pl.ds(own_y, 8))

    def there(dy):
        return pl.ds(own_y, 8) if pair else pl.ds(8 - 8 * dy, 8)

    def here_from(dy):
        if pair:
            return pl.ds(own_y if dy == 0 else pl.multiple_of((1 - me_y) * 8, 8), 8)
        return pl.ds(8 - 8 * dy, 8)

    def exists(dx, dy):
        to_x, to_y = me_x + dx, me_y + dy
        return (to_x >= 0) & (to_x < n_gx) & (to_y >= 0) & (to_y < n_gy)

    def device(dx, dy):
        return {"gx": jnp.clip(me_x + dx, 0, n_gx - 1), "gy": jnp.clip(me_y + dy, 0, n_gy - 1)}

    def copy(src, dst, send, recv, spot, side):
        return pltpu.make_async_remote_copy(
            src_ref=src, dst_ref=dst, send_sem=send.at[spot], recv_sem=recv.at[spot],
            device_id=device(*side), device_id_type=MESH,
        )

    def start(copies, sides):
        for one, (dx, dy) in zip(copies, sides):
            pl.when(exists(dx, dy))(one.start)

    def receive(copies, sides):
        for one, (dx, dy) in zip(copies, sides):
            pl.when(exists(-dx, -dy))(one.wait_recv)

    def sent(copies, sides):
        for one, (dx, dy) in zip(copies, sides):
            pl.when(exists(dx, dy))(one.wait_send)

    loads = [
        pltpu.make_async_copy(src, dst, send_in.at[spot])
        for spot, (src, dst) in enumerate(
            (
                (guess_hbm, rim.at[pl.ds(1, 8)]),
                (guess_hbm, guess.at[:, pl.ds(8, 8)]),
                (gas_hbm, wide.at[:, pl.ds(2, 8)]),
                (gas_hbm, tall.at[:, :, pl.ds(8, 8)]),
                (cell_hbm, cell),
                (motion_hbm, motion),
                (size_hbm, size),
                (target_hbm, target),
                (on_hbm, spray_on),
                (time_hbm, spray_time),
                (place_hbm, spray_cell),
            )
        )
    ]
    for one in loads:
        one.start()

    barrier = pltpu.get_barrier_semaphore()
    for dx, dy in AROUND:
        @pl.when(exists(dx, dy))
        def _():
            pl.semaphore_signal(barrier, inc=1, device_id=device(dx, dy), device_id_type=MESH)

    @pl.when(~exists(-1, 0))
    def _():
        wide[:, 0:2] = jnp.zeros((5, 2, 8, 256), F32)
        rim[0] = jnp.zeros((8, 256), F32)
        u_halo[0] = jnp.zeros((8, 256), F32)

    @pl.when(~exists(1, 0))
    def _():
        wide[:, 10:12] = jnp.zeros((5, 2, 8, 256), F32)
        rim[9] = jnp.zeros((8, 256), F32)
        u_halo[1] = jnp.zeros((8, 256), F32)

    @pl.when(~exists(0, -1))
    def _():
        edge_recv[0] = jnp.zeros((5, 8, 2, 256), F32)
        side_recv[0] = jnp.zeros((8, 1, 256), F32)
        v_recv[0] = jnp.zeros((8, 1, 256), F32)

    @pl.when(~exists(0, 1))
    def _():
        edge_recv[1] = jnp.zeros((5, 8, 2, 256), F32)
        side_recv[1] = jnp.zeros((8, 1, 256), F32)
        v_recv[1] = jnp.zeros((8, 1, 256), F32)

    for way, (dx, dy) in enumerate(SIDES):
        @pl.when(~exists(-dx, -dy))
        def _():
            landed[way] = jnp.zeros((8, 512), F32)
            if dy == 0 or not pair:
                spot = (pl.ds(8 - 8 * dx, 8), here_from(dy))
                sums[spot] = jnp.zeros((8, 8, 256), F32)
                parts[spot] = jnp.zeros((8, 8, 256), F32)

    for way, (dx, dy) in enumerate(CORNERS):
        @pl.when(~exists(-dx, -dy))
        def _():
            corner_recv[0, way] = jnp.zeros((4, 8, 256), F32)
            corner_recv[1, way] = jnp.zeros((4, 8, 256), F32)

    low_x, high_x = exists(-1, 0).astype(F32), exists(1, 0).astype(F32)
    if pair:
        factors = [low_x * (1.0 / 6.0), 1.0 / 6.0, high_x * (1.0 / 6.0)]
    else:
        row = lax.broadcasted_iota(jnp.int32, (1, tall_rows, 256), 1)
        low_y, high_y = exists(0, -1).astype(F32), exists(0, 1).astype(F32)
        factor = jnp.where(row < 8, low_y, jnp.where(row < 16, 1.0, high_y)) * (1.0 / 6.0)
        factors = [factor * low_x, factor, factor * high_x]
    summed[...] = jnp.zeros_like(summed)
    packed[...] = jnp.zeros_like(packed)

    for one in loads[0:4]:
        one.wait()
    side_send[0] = rim[1:9, 7:8]
    side_send[1] = rim[1:9, 0:1]
    for f in range(5):
        inner = wide[f, 2:10]
        edge_send[0, f] = inner[:, 6:8]
        edge_send[1, f] = inner[:, 0:2]
    pl.semaphore_wait(barrier, sum(exists(dx, dy).astype(jnp.int32) for dx, dy in AROUND))
    border = [
        copy(rim.at[8], rim.at[0], send_rim, recv_rim, 0, SIDES[0]),
        copy(rim.at[1], rim.at[9], send_rim, recv_rim, 1, SIDES[1]),
        copy(side_send.at[0], side_recv.at[0], send_rim, recv_rim, 2, SIDES[2]),
        copy(side_send.at[1], side_recv.at[1], send_rim, recv_rim, 3, SIDES[3]),
    ]
    start(border, SIDES)
    halo = [
        copy(wide.at[:, pl.ds(8, 2)], wide.at[:, pl.ds(0, 2)], send_halo, recv_halo, 0, SIDES[0]),
        copy(wide.at[:, pl.ds(2, 2)], wide.at[:, pl.ds(10, 2)], send_halo, recv_halo, 1, SIDES[1]),
        copy(edge_send.at[0], edge_recv.at[0], send_halo, recv_halo, 2, SIDES[2]),
        copy(edge_send.at[1], edge_recv.at[1], send_halo, recv_halo, 3, SIDES[3]),
    ]
    start(halo, SIDES)

    high, low = split(wide[0:4, 2:10].reshape(4 * rows, depth))
    grid_pieces[...] = jnp.concatenate([high, low], axis=0).astype(BF16)
    for one in loads[4:]:
        one.wait()

    def exchange(turn):
        here = slice(turn * CHUNK, turn * CHUNK + CHUNK)
        cells = cell[:, here]
        goal = target[:, here]
        diameter = size[:, here]
        moving = motion[:, 0, here]
        at_z = jnp.bitwise_and(cells, depth - 1)
        at_xy = lax.shift_right_logical(cells, 8)
        hot_z = (lax.broadcasted_iota(jnp.int32, (depth, CHUNK), 0) == at_z).astype(F32).astype(BF16)
        hot_xy = (lax.broadcasted_iota(jnp.int32, (rows, CHUNK), 0) == at_xy).astype(F32)
        found = jnp.dot(grid_pieces[0:256], hot_z, preferred_element_type=F32) + jnp.dot(
            grid_pieces[256:512], hot_z, preferred_element_type=F32
        )
        local = jnp.concatenate(
            [jnp.sum(found[f * rows : (f + 1) * rows] * hot_xy, axis=0, keepdims=True) for f in range(4)], axis=0
        )
        gap = local - moving
        field = lax.broadcasted_iota(jnp.int32, gap.shape, 0)
        pace = jnp.where(field == 3, TIME_STEP / HEAT_TIME, TIME_STEP / DRAG_TIME)
        fall = jnp.where(field == 2, TIME_STEP * GRAVITY, 0.0)
        carried = moving + pace * gap - fall
        vapour = VAPOUR_RATE * diameter * (1.0 / (1.0 + jnp.exp(-gap[3:4])))
        fresh = jnp.concatenate([carried, diameter - TIME_STEP * vapour], axis=0)
        renewed[0:5, here] = fresh
        kept[:, 0, here] = jnp.where(goal == 4, fresh, 0.0)
        alive = goal >= 0
        drag = jnp.where(alive, -DRAG_COUPLING * diameter * diameter * gap[2:3], 0.0)
        vapour = jnp.where(alive, vapour, 0.0)
        drag_high, drag_low = split(drag)
        vapour_high, vapour_low = split(vapour)
        spread = jnp.concatenate(
            [hot_xy * drag_high, hot_xy * vapour_high, hot_xy * drag_low, hot_xy * vapour_low], axis=0
        ).astype(BF16)
        summed[...] += lax.dot_general(spread, hot_z, NT, preferred_element_type=F32)

    turns = slots // CHUNK
    exchange(0)

    tile_row = lax.broadcasted_iota(jnp.int32, (8, 256), 0)

    def layer(dx, i):
        return 8 - i if dx > 0 else i - 1

    def blocks(buffer, which, send, recv):
        copies = [
            copy(buffer.at[own], buffer.at[pl.ds(8 - 8 * dx, 8), there(dy)], send, recv, spot, (dx, dy))
            for spot, (dx, dy) in enumerate(SIDES)
        ]
        start(copies[2:] + copies[:2], SIDES[2:] + SIDES[:2])
        block = buffer[own]
        for way, (dx, dy) in enumerate(CORNERS):
            for i in range(1, 5):
                near, far = block[layer(dx, i)], block[layer(dx, 9 - i)]
                if i > 1:
                    if dy > 0:
                        near = jnp.where(tile_row >= i, near, pltpu.roll(far, i - 1, 0))
                    else:
                        near = jnp.where(tile_row < 8 - i, near, pltpu.roll(far, 9 - i, 0))
                corner_send[which, way, i - 1] = near
        corners = [
            copy(corner_send.at[which, way], corner_recv.at[which, way], send, recv, 4 + way, side)
            for way, side in enumerate(CORNERS)
        ]
        start(corners, CORNERS)
        return copies + corners

    def unpack(buffer, which):
        for way, (dx, dy) in enumerate(CORNERS):
            def place():
                base, side = 8 - 8 * dx, here_from(dy)
                for i in range(1, 5):
                    tile = corner_recv[which, way, i - 1]
                    buffer[base + layer(dx, i), side] = tile
                    back = (9 - i if dy > 0 else i - 1) % 8
                    buffer[base + layer(dx, 9 - i), side] = pltpu.roll(tile, back, 0) if back else tile

            if pair:
                pl.when(exists(0, -dy))(place)
            else:
                place()

    receive(border, SIDES)
    guess[:, 7:8] = side_recv[0]
    guess[:, 16:17] = side_recv[1]
    sums[own] = (
        rim[2:10] + rim[0:8] + guess[:, 9:17] + guess[:, 7:15]
        + along_depth(rim[1:9], 1) + along_depth(rim[1:9], -1)
    )
    sum_copies = blocks(sums, 0, send_sum, recv_sum)

    for turn in range(1, turns // 2):
        exchange(turn)

    receive(halo, SIDES)
    for f in range(5):
        tall[f, :, 6:8] = edge_recv[0, f]
        tall[f, :, 16:18] = edge_recv[1, f]
    def predict(f):
        centre = wide[f, 2:10]
        near_x, near_x2 = wide[f, 3:11], wide[f, 1:9]
        near_y, near_y2 = tall[f, :, 9:17], tall[f, :, 7:15]
        near_z, near_z2 = along_depth(centre, -1), along_depth(centre, 1)
        laplace = near_x + near_x2 + near_y + near_y2 + near_z + near_z2 - 6.0 * centre
        slope_x = 8.0 * (near_x - near_x2) - (wide[f, 4:12] - wide[f, 0:8])
        slope_y = 8.0 * (near_y - near_y2) - (tall[f, :, 10:18] - tall[f, :, 6:14])
        slope_z = 8.0 * (near_z - near_z2) - (along_depth(centre, -2) - along_depth(centre, 2))
        transport = (wide[0, 2:10] * slope_x + wide[1, 2:10] * slope_y + wide[2, 2:10] * slope_z) * (1.0 / 12.0)
        star[f] = centre + TIME_STEP * (DIFFUSION * laplace - transport)

    for f in range(3):
        predict(f)
        if f == 1:
            tall_v[:, 8:16] = star[1]
            v_send[0] = star[1, :, 7:8]
            v_send[1] = star[1, :, 0:1]
            u_halo[2] = star[0, 7]
            u_halo[3] = star[0, 0]
            edges = [
                copy(u_halo.at[2], u_halo.at[0], send_star, recv_star, 0, SIDES[0]),
                copy(u_halo.at[3], u_halo.at[1], send_star, recv_star, 1, SIDES[1]),
                copy(v_send.at[0], v_recv.at[0], send_star, recv_star, 2, SIDES[2]),
                copy(v_send.at[1], v_recv.at[1], send_star, recv_star, 3, SIDES[3]),
            ]
            start(edges, SIDES)

    numbers = lax.broadcasted_iota(jnp.int32, (rows, depth), 0) * depth + lax.broadcasted_iota(
        jnp.int32, (rows, depth), 1
    )
    ramp = jnp.clip((CLOCK - spray_time[...].astype(F32)) / SPRAY_RAMP, 0.0, 1.0)
    strength = SPRAY_RATE * ramp * spray_on[...].astype(F32)
    spray = jnp.zeros((rows, depth), F32)
    for head in range(spray_on.shape[1]):
        spray += jnp.where(numbers == spray_cell[:, head : head + 1], strength[:, head : head + 1], 0.0)
    for turn in range(max(1, turns // 2), turns):
        exchange(turn)

    total = summed[...]
    drag = total[:rows] + total[2 * rows : 3 * rows]
    vapour = total[rows : 2 * rows] + total[3 * rows :]
    lift = star[2] + (TIME_STEP * (drag - spray)).reshape(8, 8, 256)
    star[2] = lift

    receive(edges, SIDES)
    tall_v[:, 7:8] = v_recv[0]
    tall_v[:, 16:17] = v_recv[1]
    speed = star[0]
    spread_x = jnp.concatenate([speed[1:8], u_halo[1:2]], axis=0) - jnp.concatenate(
        [u_halo[0:1], speed[0:7]], axis=0
    )
    spread = spread_x + (tall_v[:, 9:17] - tall_v[:, 7:15]) + (along_depth(lift, -1) - along_depth(lift, 1))
    parts[own] = spread * (0.5 / TIME_STEP)
    part_copies = blocks(parts, 1, send_src, recv_src)

    predict(3)
    predict(4)
    star[3] = star[3] + (TIME_STEP * (-LATENT * vapour - spray)).reshape(8, 8, 256)
    star[4] = star[4] + (TIME_STEP * vapour).reshape(8, 8, 256)

    early = [
        pltpu.make_async_copy(star.at[pl.ds(3, 2)], gas_next.at[pl.ds(3, 2)], send_out.at[0]),
        pltpu.make_async_copy(kept, kept_hbm, send_out.at[1]),
    ]
    for one in early:
        one.start()

    upper = (
        lax.broadcasted_iota(jnp.int32, (256, 256), 0) <= lax.broadcasted_iota(jnp.int32, (256, 256), 1)
    ).astype(F32).astype(BF16)
    eight = lax.broadcasted_iota(jnp.int32, (8, 256), 0)

    def pack(turn, carry):
        here = slice(turn * CHUNK, turn * CHUNK + CHUNK)
        goal = target[:, here]
        pieces = [(eight == goal[:, k * 256 : k * 256 + 256]).astype(F32) for k in range(CHUNK // 256)]
        counts = jnp.dot(jnp.concatenate(pieces, axis=0).astype(BF16), upper, preferred_element_type=F32)
        places = []
        for k, piece in enumerate(pieces):
            count = counts[8 * k : 8 * k + 8] + carry
            carry = count[:, 255:256]
            place = jnp.where(eight < 4, piece * (count + (512.0 * eight.astype(F32))), 0.0)
            places.append(jnp.sum(place, axis=0, keepdims=True))
        place = jnp.concatenate(places, axis=1).astype(jnp.int32) - 1
        hot_low = (
            lax.broadcasted_iota(jnp.int32, (256, CHUNK), 0) == jnp.bitwise_and(place, 255)
        ).astype(F32).astype(BF16)
        hot_high = (
            lax.broadcasted_iota(jnp.int32, (8, CHUNK), 0) == lax.shift_right_arithmetic(place, 8)
        ).astype(F32)
        top, rest = split(renewed[0:5, here])
        bundle = jnp.concatenate(
            [hot_high * top[f : f + 1] for f in range(5)] + [hot_high * rest[f : f + 1] for f in range(5)], axis=0
        ).astype(BF16)
        packed[...] += lax.dot_general(bundle, hot_low, NT, preferred_element_type=F32)
        return carry

    carry = jnp.zeros((8, 1), F32)
    for turn in range(turns):
        carry = pack(turn, carry)
    bundle = packed[0:40] + packed[40:80]
    for f in range(5):
        for way in range(4):
            for half in range(2):
                spot = f * 8 + 2 * way + half
                parcels[way, f : f + 1, half * 256 : half * 256 + 256] = bundle[spot : spot + 1]
    for way in range(4):
        parcels[way, 5:8] = jnp.zeros((3, 512), F32)
    parcel = [
        copy(parcels.at[way], landed.at[way], send_parcel, recv_parcel, way, SIDES[way]) for way in range(4)
    ]
    start(parcel, SIDES)

    receive(sum_copies, AROUND)
    unpack(sums, 0)
    receive(part_copies, AROUND)
    unpack(parts, 1)

    for x in range(0, 24, 4):
        swap[0, x : x + 4] = (sums[x : x + 4] - parts[x : x + 4]) * factors[x // 8]
    for turn in range(1, ITERS):
        old, new = swap.at[(turn - 1) % 2], swap.at[turn % 2]
        x = turn
        while x < 24 - turn:
            end = min(x + (4 if pair else 2), 24 - turn, (x // 8 + 1) * 8)
            centre = old[x:end]
            total = old[x - 1 : end - 1] + old[x + 1 : end + 1]
            total = total + along_rows(centre, 1) + along_rows(centre, -1)
            total = total + along_depth(centre, 1) + along_depth(centre, -1)
            new[x:end] = (total - parts[x:end]) * factors[x // 8]
            x = end

    last = swap.at[(ITERS - 1) % 2]
    centre = last[own]
    final[...] = centre
    half = TIME_STEP * 0.5
    star[0] = star[0] - half * (last[9:17, pl.ds(own_y, 8)] - last[7:15, pl.ds(own_y, 8)])
    star[2] = star[2] - half * (along_depth(centre, -1) - along_depth(centre, 1))
    middle = last[8:16]
    spare = swap.at[ITERS % 2]
    spare[8:16] = along_rows(middle, -1) - along_rows(middle, 1)
    star[1] = star[1] - half * spare[own]
    late = [
        pltpu.make_async_copy(star.at[pl.ds(0, 3)], gas_next.at[pl.ds(0, 3)], send_out.at[2]),
        pltpu.make_async_copy(final, pressure, send_out.at[3]),
    ]
    for one in late:
        one.start()
    receive(parcel, SIDES)
    for way in range(4):
        arrived[way, :, 0, :] = landed[way, 0:5]
    late.append(pltpu.make_async_copy(arrived, arrived_hbm, send_out.at[4]))
    late[2].start()

    sent(border, SIDES)
    sent(halo, SIDES)
    sent(edges, SIDES)
    sent(sum_copies, AROUND)
    sent(part_copies, AROUND)
    sent(parcel, SIDES)
    for one in early + late:
        one.wait()


def hand_over_kernel(*refs):
    sems = refs[-1]
    into = [pltpu.make_async_copy(refs[k], refs[8 + k], sems.at[k]) for k in range(4)]
    out = [pltpu.make_async_copy(refs[8 + k], refs[4 + k], sems.at[4 + k]) for k in range(4)]
    for one in into:
        one.start()
    for k in (3, 1, 2, 0):
        into[k].wait()
        out[k].start()
    for one in out:
        one.wait()


def body(
    n_gx, n_gy,
    gas_state, pressure_guess, drop_motion, drop_size, drop_cell, drop_target, spray_on, spray_time, spray_cell,
):
    hbm = pl.BlockSpec(memory_space=pltpu.HBM)
    dma = pltpu.SemaphoreType.DMA
    slots = drop_size.shape[1]
    heads = spray_on.shape[1]
    tall_rows = 16 if n_gy == 2 else 24
    block = gas_state.shape[1:]
    shape = functools.partial(jax.ShapeDtypeStruct, dtype=F32)
    outs = (shape(gas_state.shape), shape(block), shape((5, 1, slots)), shape((4, 5, 1, 512)))
    results = pl.pallas_call(
        functools.partial(evolve_kernel, n_gx, n_gy),
        out_shape=outs,
        in_specs=[hbm] * 9,
        out_specs=(hbm,) * 4,
        scratch_shapes=[
            pltpu.VMEM(gas_state.shape, F32),
            pltpu.VMEM((5, 1, slots), F32),
            pltpu.VMEM((4, 5, 1, 512), F32),
            pltpu.VMEM((2, 24, tall_rows, 256), F32),
            pltpu.VMEM(block, F32),
            pltpu.VMEM(drop_motion.shape, F32),
            pltpu.VMEM((1, slots), F32),
            pltpu.VMEM((1, slots), jnp.int32),
            pltpu.VMEM((1, slots), jnp.int32),
            pltpu.VMEM((1, heads), jnp.int32),
            pltpu.VMEM((1, heads), jnp.int32),
            pltpu.VMEM((1, heads), jnp.int32),
            pltpu.VMEM((512, 256), BF16),
            pltpu.VMEM((256, 256), F32),
            pltpu.VMEM((80, 256), F32),
            pltpu.VMEM((8, slots), F32),
            pltpu.VMEM((4, 8, 512), F32),
            pltpu.VMEM((4, 8, 512), F32),
            pltpu.VMEM((8, 24, 256), F32),
            pltpu.VMEM((10, 8, 256), F32),
            pltpu.VMEM((2, 8, 1, 256), F32),
            pltpu.VMEM((2, 8, 1, 256), F32),
            pltpu.VMEM((5, 12, 8, 256), F32),
            pltpu.VMEM((5, 8, 24, 256), F32),
            pltpu.VMEM((2, 5, 8, 2, 256), F32),
            pltpu.VMEM((2, 5, 8, 2, 256), F32),
            pltpu.VMEM((24, tall_rows, 256), F32),
            pltpu.VMEM((24, tall_rows, 256), F32),
            pltpu.VMEM((2, 4, 4, 8, 256), F32),
            pltpu.VMEM((2, 4, 4, 8, 256), F32),
            pltpu.VMEM((8, 24, 256), F32),
            pltpu.VMEM((4, 8, 256), F32),
            pltpu.VMEM((2, 8, 1, 256), F32),
            pltpu.VMEM((2, 8, 1, 256), F32),
        ]
        + [dma((11,)), dma((5,))] + [dma((4,))] * 8 + [dma((8,))] * 4,
        compiler_params=pltpu.CompilerParams(
            collective_id=0, has_side_effects=True, vmem_limit_bytes=60 * 1024 * 1024
        ),
    )(
        gas_state, pressure_guess, drop_motion, drop_size, drop_cell, drop_target, spray_on, spray_time, spray_cell
    )
    return pl.pallas_call(
        hand_over_kernel,
        out_shape=outs,
        in_specs=[hbm] * 4,
        out_specs=(hbm,) * 4,
        scratch_shapes=[pltpu.VMEM(one.shape, F32) for one in outs] + [dma((8,))],
        compiler_params=pltpu.CompilerParams(vmem_limit_bytes=60 * 1024 * 1024),
    )(*results)


def solution(mesh):
    in_specs = (
        P(None, "gx", "gy", None),
        P("gx", "gy", None),
        P(None, "gx", "gy"),
    ) + (P("gx", "gy"),) * 6
    out_specs = (
        P(None, "gx", "gy", None),
        P("gx", "gy", None),
        P(None, "gx", "gy"),
        P(None, None, "gx", "gy"),
    )
    inner = functools.partial(body, mesh.shape["gx"], mesh.shape["gy"])
    return jax.shard_map(inner, mesh=mesh, in_specs=in_specs, out_specs=out_specs, check_vma=False)
```
